128 devices in a mesh: lat: 8 (over z, x_lo), lon: 16 (over y, x_hi, core).
Axes of the slice: x: 4 (x_hi: 2, x_lo: 2; x = x_hi * 2 + x_lo), y: 4, z: 4, core: 2. Of those that a mesh axis runs over, the one named last changes fastest.
Arguments:
- latents: bfloat16 [2, 96, 576, 1024], P(None, 'lat', None, 'lon'), may hold values from -6 to 6
- land_mask: int32 [2, 96, 576], P(None, 'lat'), may hold values 0 or 1
- norm_gain: float32 [1024], replicated, may hold values from 0.5 to 5
- qkv_weight: bfloat16 [1024, 3072], replicated, may hold values from -0.1875 to 0.1875
- out_weight: bfloat16 [1024, 1024], replicated, may hold values from -0.1875 to 0.1875
- out_cotangent: bfloat16 [2, 96, 576, 1024], P(None, 'lat', 'lon'), may hold values from -6 to 6
Outputs:
- block_out: bfloat16 [2, 96, 576, 1024], P(None, 'lat', 'lon')
- latent_grad: bfloat16 [2, 96, 576, 1024], P(None, 'lat', None, 'lon')
- qkv_weight_grad: float32 [1024, 3072], P(('lat', 'lon'))
- out_weight_grad: float32 [1024, 1024], P(('lat', 'lon'))
- gain_grad: float32 [1024], P(('lat', 'lon'))
The draws below stay inside these ranges and needn't reach their ends.
Inputs may be any that keep to these rules, and one draw needn't show every extreme that they name: `land_mask`: 1 marks land.
All inputs are finite; a program needn't handle non-finite values. No bound on the sum of `land_mask` on one device may be relied on, other than what follows from the above.
Results may differ from the reference program's by a relative error of at most 0.0085.
The reference program's roundings to bfloat16 on the way (of `rolled`, `scaled`, `projected`, `prob_half`, `attended`, `out_grad`, `score_grad` and `qkv_grad`) count: a program that leaves them out, or rounds other values in their place, can miss the bound.
Values may be sent and summed in bfloat16 or wider, within the bound.
No kernel may reach another device: no remote copies, remote signals or barrier semaphores. Data moves between devices by JAX's collectives and lax.ppermute only.
A program may use at most 192 MiB of HBM per device.

```python
import jax
import jax.numpy as jnp
from jax import lax

D = 1024
HEADS = 16
LEVELS = 2
WLAT = 6
WLON = 12
SHIFT = 6
WIN_LON_DEV = 3
LAT = 96
LON = 576


def draw_norm_gain(key, part):
    key = jax.random.fold_in(key, 7)
    return jax.random.uniform(key, (D,), jnp.float32, 0.5, 1.5)


def place_ends(values, rng, low, top_value):
    longest = values.shape.index(max(values.shape))
    spots = []
    for shift in (0, 1):
        where = [jax.random.randint(jax.random.fold_in(rng, axis), (), 0, length) for axis, length in enumerate(values.shape)]
        where[longest] = (where[longest] + shift) % values.shape[longest]
        spots.append(tuple(where))
    return values.at[spots[0]].set(low).at[spots[1]].set(top_value)


def steps_of(key, extent, cuts, low, high):
    level, own = 1.0, jax.random.fold_in(key, 6)
    for axis_at, blocks in cuts:
        draws = jnp.exp(jax.random.uniform(jax.random.fold_in(own, axis_at), (blocks,), jnp.float32, low / len(cuts), high / len(cuts)))
        level = level * jnp.repeat(draws, extent[axis_at] // blocks).reshape([-1 if axis == axis_at else 1 for axis in range(len(extent))])
    return level


def gaussian(key, extent, width, limit, split=(), kind=jnp.bfloat16):
    factor_of = steps_of(key, extent, split, -0.22, 0.18) if split else 1.0
    entries = jax.random.normal(key, extent, jnp.float32) * width * factor_of
    return jnp.minimum(jnp.maximum(entries, -limit), limit).astype(kind)


def setup_inputs(seed: int = 0) -> dict:
    keys = jax.random.split(jax.random.key(seed), 7)
    return {
        "latents": gaussian(keys[0], (LEVELS, LAT, LON, D), 1.0, 6.0, ((1, 8), (3, 16))),
        "land_mask": place_ends((jax.random.randint(keys[1], (LEVELS, LAT, LON), 0, 2) < 1).astype(jnp.int32), jax.random.fold_in(keys[1], 1), 0, 1),
        "norm_gain": draw_norm_gain(jax.random.fold_in(keys[6], 71), 0),
        "qkv_weight": gaussian(keys[3], (D, 3 * D), D ** -0.5, 0.1875),
        "out_weight": gaussian(keys[4], (D, D), D ** -0.5, 0.1875),
        "out_cotangent": gaussian(keys[5], (LEVELS, LAT, LON, D), 1.0, 6.0, ((1, 8), (2, 16))),
    }


def layer_norm(flat):
    values_f = flat.astype(jnp.float32)
    centred = values_f - lax.optimization_barrier(jnp.mean(values_f, axis=-1, keepdims=True))
    variance = lax.optimization_barrier(jnp.mean(centred * centred, axis=-1, keepdims=True))
    inv_scale = lax.rsqrt(variance + 1e-05)
    return (centred * inv_scale, inv_scale)

def to_windows(grid):
    levels, lat_rows, lon_cols, feat_dim = grid.shape
    grid = grid.reshape(levels, lat_rows // WLAT, WLAT, lon_cols // WLON, WLON, feat_dim)
    grid = grid.transpose(1, 3, 0, 2, 4, 5)
    return grid.reshape(-1, levels * WLAT * WLON, feat_dim)

def from_windows(windows, levels, lat_rows, lon_cols):
    feat_dim = windows.shape[-1]
    grid = windows.reshape(lat_rows // WLAT, lon_cols // WLON, levels, WLAT, WLON, feat_dim)
    return grid.transpose(2, 0, 3, 1, 4, 5).reshape(levels, lat_rows, lon_cols, feat_dim)

def window_pass(projected, upstream, mask_win):
    batch, win_tokens, triple = projected.shape
    feat_dim = triple // 3
    head_dim = feat_dim // HEADS
    factor = head_dim ** (-0.5)
    queries = projected[..., :feat_dim].reshape(batch, win_tokens, HEADS, head_dim).astype(jnp.float32)
    key_rows = projected[..., feat_dim:2 * feat_dim].reshape(batch, win_tokens, HEADS, head_dim).astype(jnp.float32)
    value_rows = projected[..., 2 * feat_dim:].reshape(batch, win_tokens, HEADS, head_dim).astype(jnp.float32)
    scores = jnp.einsum('bqhe,bkhe->bhqk', queries, key_rows) * factor
    allowed = (mask_win[:, None, None, :] == 1) | jnp.eye(win_tokens, dtype=bool)[None, None]
    scores = jnp.where(allowed, scores, -jnp.inf)
    highest = lax.optimization_barrier(jnp.max(scores, axis=-1, keepdims=True))
    raised = jnp.exp(scores - highest)
    prob_full = raised / lax.optimization_barrier(jnp.sum(raised, axis=-1, keepdims=True))
    prob_half = prob_full.astype(jnp.bfloat16).astype(jnp.float32)
    attended = jnp.einsum('bhqk,bkhe->bqhe', prob_half, value_rows).reshape(batch, win_tokens, feat_dim)
    attended = attended.astype(jnp.bfloat16)
    grad_heads = upstream.reshape(batch, win_tokens, HEADS, head_dim).astype(jnp.float32)
    prob_grad = jnp.einsum('bqhe,bkhe->bhqk', grad_heads, value_rows)
    inner = lax.optimization_barrier(jnp.sum(prob_full * prob_grad, axis=-1, keepdims=True))
    score_grad = (prob_full * (prob_grad - inner) * factor).astype(jnp.bfloat16).astype(jnp.float32)
    query_grad = jnp.einsum('bhqk,bkhe->bqhe', score_grad, key_rows)
    key_grad = jnp.einsum('bhqk,bqhe->bkhe', score_grad, queries)
    value_grad = jnp.einsum('bhqk,bqhe->bkhe', prob_half, grad_heads)
    qkv_grad = jnp.concatenate([query_grad.reshape(batch, win_tokens, feat_dim), key_grad.reshape(batch, win_tokens, feat_dim), value_grad.reshape(batch, win_tokens, feat_dim)], axis=-1)
    return (attended, qkv_grad.astype(jnp.bfloat16))

def reference(latents, land_mask, norm_gain, qkv_weight, out_weight, out_cotangent):
    rolled = jnp.roll(latents, -SHIFT, axis=2)
    mask_rolled = jnp.roll(land_mask, -SHIFT, axis=2)
    levels, lat_rows, lon_cols, feat_dim = rolled.shape
    flat = rolled.reshape(-1, feat_dim)
    normed, inv_scale = layer_norm(flat)
    scaled = (normed * norm_gain).astype(jnp.bfloat16)
    projected = jnp.dot(scaled, qkv_weight, preferred_element_type=jnp.float32).astype(jnp.bfloat16)
    upstream_flat = out_cotangent.reshape(-1, feat_dim)
    out_grad = jnp.dot(upstream_flat, out_weight.T, preferred_element_type=jnp.float32).astype(jnp.bfloat16)
    qkv_win = to_windows(projected.reshape(levels, lat_rows, lon_cols, 3 * feat_dim))
    grad_win = to_windows(out_grad.reshape(levels, lat_rows, lon_cols, feat_dim))
    mask_win = to_windows(mask_rolled[..., None])[..., 0]
    win_count, win_tokens = mask_win.shape
    groups = win_count // WIN_LON_DEV
    qkv_win = qkv_win.reshape(groups, WIN_LON_DEV, win_tokens, 3 * feat_dim)
    grad_win = grad_win.reshape(groups, WIN_LON_DEV, win_tokens, feat_dim)
    mask_win = mask_win.reshape(groups, WIN_LON_DEV, win_tokens)
    attended, qkv_grad = lax.map(lambda item: window_pass(item[0], item[1], item[2]), (qkv_win, grad_win, mask_win))
    attended = from_windows(attended.reshape(-1, win_tokens, feat_dim), levels, lat_rows, lon_cols).reshape(-1, feat_dim)
    qkv_grad = from_windows(qkv_grad.reshape(-1, win_tokens, 3 * feat_dim), levels, lat_rows, lon_cols).reshape(-1, 3 * feat_dim)
    block_out = (flat.astype(jnp.float32) + jnp.dot(attended, out_weight, preferred_element_type=jnp.float32)).astype(jnp.bfloat16)
    block_out = block_out.reshape(levels, lat_rows, lon_cols, feat_dim)
    out_weight_grad = jnp.dot(attended.T, upstream_flat, preferred_element_type=jnp.float32)
    qkv_weight_grad = jnp.dot(scaled.T, qkv_grad, preferred_element_type=jnp.float32)
    norm_grad = jnp.dot(qkv_grad, qkv_weight.T, preferred_element_type=jnp.float32)
    gain_grad = lax.optimization_barrier(jnp.sum(norm_grad * normed, axis=0))
    scaled_grad = norm_grad * norm_gain
    input_grad = inv_scale * (scaled_grad - lax.optimization_barrier(jnp.mean(scaled_grad, axis=-1, keepdims=True)) - normed * lax.optimization_barrier(jnp.mean(scaled_grad * normed, axis=-1, keepdims=True)))
    latent_grad = (upstream_flat.astype(jnp.float32) + input_grad).astype(jnp.bfloat16)
    latent_grad = jnp.roll(latent_grad.reshape(levels, lat_rows, lon_cols, feat_dim), SHIFT, axis=2)
    return (block_out, latent_grad, qkv_weight_grad, out_weight_grad, gain_grad)
```

```python
import functools

import jax
import jax.numpy as jnp
from jax import lax
from jax.experimental import pallas as pl
from jax.experimental.pallas import tpu as pltpu
from jax.sharding import PartitionSpec as P

F32 = jnp.float32
BF16 = jnp.bfloat16
D = 1024
HEAD = 64
WIN = 144
HALF = 72
WINS = 6
TOK = WIN * WINS
SHIFT = 6
LON = 576
GROUPS = 4
GW = D // GROUPS
SCALE = HEAD**-0.5
LOG2E = 1.4426950408889634
MIB = 1 << 20
AXES = ("lat", "lon")


def nn(a, b):
    return lax.dot_general(a, b, (((1,), (0,)), ((), ())), preferred_element_type=F32)


def nt(a, b):
    return lax.dot_general(a, b, (((1,), (1,)), ((), ())), preferred_element_type=F32)


def params(mib):
    return pltpu.CompilerParams(vmem_limit_bytes=mib * MIB)


def cost(flops, nbytes):
    return pl.CostEstimate(flops=int(flops), bytes_accessed=int(nbytes), transcendentals=0)


def vmem(n):
    return [pl.BlockSpec(memory_space=pltpu.VMEM)] * n


def split_kernel(z_ref, out_ref, t_ref, s_ref):
    row = lax.broadcasted_iota(jnp.int32, (LON, LON), 0)
    col = lax.broadcasted_iota(jnp.int32, (LON, LON), 1)
    source = row + SHIFT
    source = jnp.where(source >= LON, source - LON, source)
    pick = (col == source).astype(BF16)
    for r in range(12):
        both = jnp.concatenate([z_ref[0, r], z_ref[1, r]], axis=0)
        t_ref[...] = nt(pick, both)
        for v in range(48):
            at = ((r // 6) * 3 + v % 3) * HALF + (r % 6) * 12
            s_ref[v // 3, at : at + 12, :] = t_ref[12 * v : 12 * v + 12, :]
    for k in range(16):
        out_ref[k] = s_ref[k].astype(BF16)


def split_pieces(z):
    return pl.pallas_call(
        split_kernel,
        out_shape=jax.ShapeDtypeStruct((16, 6 * HALF, 128), BF16),
        in_specs=vmem(1),
        out_specs=vmem(1)[0],
        scratch_shapes=[pltpu.VMEM((LON, 128), F32), pltpu.VMEM((16, 6 * HALF, 128), F32)],
        compiler_params=params(32),
        cost_estimate=cost(2e9, 4e6),
        name="split_pieces",
    )(z)


def norm_parts(x):
    centred = x - jnp.sum(x, axis=-1, keepdims=True) * (1.0 / D)
    variance = jnp.sum(centred * centred, axis=-1, keepdims=True) * (1.0 / D)
    inv_scale = lax.rsqrt(variance + 1e-05)
    return centred * inv_scale, inv_scale


def enter_kernel(r_ref, gain_ref, pick_ref, x_ref, scaled_ref, scaled_t_ref, xs_ref):
    low = lax.broadcasted_iota(jnp.int32, (6 * HALF, 128), 1) < HEAD
    for p in range(8):
        first = r_ref[2 * p].astype(F32)
        second = r_ref[2 * p + 1].astype(F32)
        level0 = jnp.where(low, first, pltpu.roll(second, HEAD, 1))
        level1 = jnp.where(low, pltpu.roll(first, HEAD, 1), second)
        for w in range(WINS):
            at = w * WIN
            xs_ref[at : at + HALF, 128 * p : 128 * p + 128] = level0[HALF * w : HALF * w + HALF]
            xs_ref[at + HALF : at + WIN, 128 * p : 128 * p + 128] = level1[HALF * w : HALF * w + HALF]

    def rows(i, _):
        at = pl.ds(pl.multiple_of(i * 48, 48), 48)
        x = xs_ref[at, :]
        x_ref[at, :] = x.astype(BF16)
        normed, _ = norm_parts(x)
        scaled_ref[at, :] = (normed * gain_ref[...]).astype(BF16)
        return 0

    lax.fori_loop(0, TOK // 48, rows, 0)

    def turn(i, _):
        at = pl.ds(pl.multiple_of(i * 256, 256), 256)
        scaled_t_ref[at, :] = nt(pick_ref[at, :], scaled_ref[...]).astype(BF16)
        return 0

    lax.fori_loop(0, 4, turn, 0)


def enter(pieces, gain, pick):
    return pl.pallas_call(
        enter_kernel,
        out_shape=(
            jax.ShapeDtypeStruct((TOK, D), BF16),
            jax.ShapeDtypeStruct((TOK, D), BF16),
            jax.ShapeDtypeStruct((D, TOK), BF16),
        ),
        in_specs=vmem(3),
        out_specs=tuple(vmem(3)),
        scratch_shapes=[pltpu.VMEM((TOK, D), F32)],
        compiler_params=params(32),
        cost_estimate=cost(3e9, 9e6),
        name="enter",
    )(pieces, gain, pick)


def attend_kernel(
    scaled_ref, scaled_t_ref, up_ref, wq_ref, wk_ref, wv_ref, wo_ref, mask_ref,
    att_ref, grad_ref, keep_ref, send_ref, q_ref, k_ref, v_ref, o_ref,
):
    for w_ref, p_ref in ((wq_ref, q_ref), (wk_ref, k_ref), (wv_ref, v_ref)):
        p_ref[...] = nn(scaled_ref[...], w_ref[...]).astype(BF16)
    o_ref[...] = nt(up_ref[...], wo_ref[...]).astype(BF16)

    same = lax.broadcasted_iota(jnp.int32, (WIN, WIN), 0) == lax.broadcasted_iota(
        jnp.int32, (WIN, WIN), 1
    )
    lane = lax.broadcasted_iota(jnp.int32, (WIN, 128), 1)
    zero = jnp.zeros((WIN, 128), BF16)

    def window(i, _):
        at = pl.ds(pl.multiple_of(i * WIN, WIN), WIN)
        bias = jnp.where(same, 0.0, mask_ref[at, :])
        for pair in range(GW // 128):
            cols = slice(128 * pair, 128 * pair + 128)
            q, k, v, o = q_ref[at, cols], k_ref[at, cols], v_ref[at, cols], o_ref[at, cols]
            k_t = (k * BF16(SCALE)).T
            v_t = v.T
            att_t, dq_t, dk, dv = [], [], None, None
            for h in range(2):
                mine = (lane < HEAD) if h == 0 else (lane >= HEAD)
                q_h = jnp.where(mine, q, zero)
                o_h = jnp.where(mine, o, zero)
                part = slice(HEAD * h, HEAD * h + HEAD)
                scores = nt(k, q_h) * (SCALE * LOG2E) + bias
                raised = jnp.exp2(scores - jnp.max(scores, axis=0, keepdims=True))
                prob = raised * (1.0 / jnp.sum(raised, axis=0, keepdims=True))
                prob_half = prob.astype(BF16)
                att_t.append(nn(v_t[part], prob_half))
                prob_grad = nt(v, o_h)
                inner = jnp.sum(prob * prob_grad, axis=0, keepdims=True)
                score_grad = (prob * (prob_grad - inner)).astype(BF16)
                dq_t.append(nn(k_t[part], score_grad))
                dk_h = nn(score_grad, q_h * BF16(SCALE))
                dv_h = nn(prob_half, o_h)
                dk = dk_h if dk is None else dk + dk_h
                dv = dv_h if dv is None else dv + dv_h
            att_ref[at, cols] = jnp.concatenate(att_t, axis=0).astype(BF16).T
            base = 128 * pair
            grad_ref[at, base : base + 128] = jnp.concatenate(dq_t, axis=0).astype(BF16).T
            grad_ref[at, GW + base : GW + base + 128] = dk.astype(BF16)
            grad_ref[at, 2 * GW + base : 2 * GW + base + 128] = dv.astype(BF16)
        return 0

    lax.fori_loop(0, WINS, window, 0)

    def weights(i, _):
        at = pl.ds(pl.multiple_of(i * 256, 256), 256)
        keep_ref[at, :] = nn(scaled_t_ref[at, :], grad_ref[...])
        far = pl.ds(pl.multiple_of(i * 256 + 512, 256), 256)
        send_ref[at, :] = nn(scaled_t_ref[far, :], grad_ref[...])
        return 0

    lax.fori_loop(0, 2, weights, 0)


def attend(g, scaled, scaled_t, up, qkv_weight, out_weight, mask):
    full = lambda shape: pl.BlockSpec(shape, lambda i: (0, 0))
    return pl.pallas_call(
        attend_kernel,
        grid=(1,),
        out_shape=(
            jax.ShapeDtypeStruct((TOK, GW), BF16),
            jax.ShapeDtypeStruct((TOK, 3 * GW), BF16),
            jax.ShapeDtypeStruct((D // 2, 3 * GW), F32),
            jax.ShapeDtypeStruct((D // 2, 3 * GW), F32),
        ),
        in_specs=[
            full((TOK, D)),
            full((D, TOK)),
            full((TOK, D)),
            pl.BlockSpec((D, GW), lambda i: (0, g)),
            pl.BlockSpec((D, GW), lambda i: (0, GROUPS + g)),
            pl.BlockSpec((D, GW), lambda i: (0, 2 * GROUPS + g)),
            pl.BlockSpec((GW, D), lambda i: (g, 0)),
            full((TOK, 1)),
        ],
        out_specs=(
            full((TOK, GW)),
            full((TOK, 3 * GW)),
            full((D // 2, 3 * GW)),
            full((D // 2, 3 * GW)),
        ),
        scratch_shapes=[pltpu.VMEM((TOK, GW), BF16)] * 4,
        compiler_params=params(48),
        cost_estimate=cost(8e9, 15e6),
        name="attend",
    )(scaled, scaled_t, up, qkv_weight, qkv_weight, qkv_weight, out_weight, mask)


def out_grad_kernel(a0, a1, a2, a3, up_ref, pick_ref, keep_ref, send_ref, t_ref):
    for g, a in enumerate((a0, a1, a2, a3)):
        piece = nt(pick_ref[:, GW * g : GW * g + GW], a[...])
        t_ref[...] = piece if g == 0 else t_ref[...] + piece

    def rows(i, _):
        at = pl.ds(pl.multiple_of(i * 256, 256), 256)
        keep_ref[at, :] = nn(t_ref[at, :].astype(BF16), up_ref[...])
        far = pl.ds(pl.multiple_of(i * 256 + 512, 256), 256)
        send_ref[at, :] = nn(t_ref[far, :].astype(BF16), up_ref[...])
        return 0

    lax.fori_loop(0, 2, rows, 0)


def out_weight_sum(att, up, pick):
    return pl.pallas_call(
        out_grad_kernel,
        out_shape=(
            jax.ShapeDtypeStruct((D // 2, D), F32),
            jax.ShapeDtypeStruct((D // 2, D), F32),
        ),
        in_specs=vmem(6),
        out_specs=tuple(vmem(2)),
        scratch_shapes=[pltpu.VMEM((D, TOK), F32)],
        compiler_params=params(40),
        cost_estimate=cost(4e9, 10e6),
        name="out_weight_sum",
    )(*att, up, pick)


def block_kernel(a0, a1, a2, a3, x_ref, w_ref, out_ref):
    def rows(i, _):
        at = pl.ds(pl.multiple_of(i * 432, 432), 432)
        total = x_ref[at, :].astype(F32)
        for g, a in enumerate((a0, a1, a2, a3)):
            total = total + nn(a[at, :], w_ref[GW * g : GW * g + GW, :])
        out_ref[at, :] = total.astype(BF16)
        return 0

    lax.fori_loop(0, 2, rows, 0)


def block_sum(att, x, out_weight):
    return pl.pallas_call(
        block_kernel,
        out_shape=jax.ShapeDtypeStruct((TOK, D), BF16),
        in_specs=vmem(6),
        out_specs=vmem(1)[0],
        compiler_params=params(32),
        cost_estimate=cost(2e9, 8e6),
        name="block_sum",
    )(*att, x, out_weight)


def leave_kernel(g0, g1, g2, g3, w_ref, x_ref, up_ref, gain_ref, out_ref, gain_out_ref, n_ref):
    def product(i, _):
        at = pl.ds(pl.multiple_of(i * 432, 432), 432)
        total = None
        for g, d in enumerate((g0, g1, g2, g3)):
            for part in range(3):
                base = part * D + g * GW
                piece = nt(d[at, part * GW : part * GW + GW], w_ref[:, base : base + GW])
                total = piece if total is None else total + piece
        n_ref[at, :] = total
        return 0

    lax.fori_loop(0, 2, product, 0)

    def rows(i, gain_sum):
        at = pl.ds(pl.multiple_of(i * 48, 48), 48)
        normed, inv_scale = norm_parts(x_ref[at, :].astype(F32))
        n = n_ref[at, :]
        both = n * normed
        gain = gain_ref[...]
        g = n * gain
        mean_g = jnp.sum(g, axis=-1, keepdims=True) * (1.0 / D)
        mean_gn = jnp.sum(both * gain, axis=-1, keepdims=True) * (1.0 / D)
        n_ref[at, :] = up_ref[at, :].astype(F32) + inv_scale * (g - mean_g - normed * mean_gn)
        return gain_sum + jnp.sum(both.reshape(6, 8, D), axis=0)

    gain_sum = lax.fori_loop(0, TOK // 48, rows, jnp.zeros((8, D), F32))
    gain_out_ref[...] = jnp.sum(gain_sum, axis=0, keepdims=True)

    low = lax.broadcasted_iota(jnp.int32, (6 * HALF, 128), 1) < HEAD
    for p in range(8):
        cols = slice(128 * p, 128 * p + 128)
        level0 = jnp.concatenate([n_ref[WIN * w : WIN * w + HALF, cols] for w in range(WINS)], axis=0)
        level1 = jnp.concatenate([n_ref[WIN * w + HALF : WIN * w + WIN, cols] for w in range(WINS)], axis=0)
        out_ref[2 * p] = jnp.where(low, level0, pltpu.roll(level1, HEAD, 1)).astype(BF16)
        out_ref[2 * p + 1] = jnp.where(low, pltpu.roll(level0, HEAD, 1), level1).astype(BF16)


def leave(grads, qkv_weight, x, up, gain):
    return pl.pallas_call(
        leave_kernel,
        out_shape=(
            jax.ShapeDtypeStruct((16, 6 * HALF, 128), BF16),
            jax.ShapeDtypeStruct((1, D), F32),
        ),
        in_specs=vmem(8),
        out_specs=tuple(vmem(2)),
        scratch_shapes=[pltpu.VMEM((TOK, D), F32)],
        compiler_params=params(44),
        cost_estimate=cost(6e9, 18e6),
        name="leave",
    )(*grads, qkv_weight, x, up, gain)


def join_kernel(r_ref, out_ref, s_ref, t_ref):
    for k in range(16):
        s_ref[k] = r_ref[k].astype(F32)
    same = lax.broadcasted_iota(jnp.int32, (128, 128), 0) == lax.broadcasted_iota(
        jnp.int32, (128, 128), 1
    )
    same = same.astype(BF16)
    for r in range(12):
        for v in range(48):
            at = ((r // 6) * 3 + v % 3) * HALF + (r % 6) * 12
            to = 12 * v + SHIFT
            if to + 12 <= LON:
                t_ref[to : to + 12, :] = s_ref[v // 3, at : at + 12, :]
            else:
                t_ref[to:LON, :] = s_ref[v // 3, at : at + LON - to, :]
                t_ref[0 : to + 12 - LON, :] = s_ref[v // 3, at + LON - to : at + 12, :]
        turned = nt(same, t_ref[...].astype(BF16)).astype(BF16)
        out_ref[0, r] = turned[:HEAD]
        out_ref[1, r] = turned[HEAD:]


def join_pieces(pieces):
    return pl.pallas_call(
        join_kernel,
        out_shape=jax.ShapeDtypeStruct((2, 12, HEAD, LON), BF16),
        in_specs=vmem(1),
        out_specs=vmem(1)[0],
        scratch_shapes=[pltpu.VMEM((16, 6 * HALF, 128), F32), pltpu.VMEM((LON, 128), F32)],
        compiler_params=params(32),
        cost_estimate=cost(2e9, 4e6),
        name="join_pieces",
    )(pieces)


def device_index(x, y, z, core):
    return ((z * 2 + x % 2) * 4 + y) * 4 + (x // 2) * 2 + core


def moved(dz=0, dx=0, dy=0, core=0):
    pairs = []
    for x in range(4):
        for y in range(4):
            for z in range(4):
                for c in range(2):
                    to = device_index((x + dx) % 4, (y + dy) % 4, (z + dz) % 4, c ^ core)
                    pairs.append((device_index(x, y, z, c), to))
    return sorted(pairs)


def ship(a, **by):
    return lax.ppermute(a, AXES, moved(**by))


def scatter_sum(keep, send, order):
    names = ["dz", "dx", "dy"]
    wide = keep.shape[-1]
    terms = [keep.reshape(4, 4, 4, 8, wide), ship(send, core=1).reshape(4, 4, 4, 8, wide)]
    for axis in order:
        at = names.index(axis)
        names.pop(at)

        def cut(d):
            total = None
            for t in terms:
                piece = lax.index_in_dim(t, d, at, keepdims=False)
                total = piece if total is None else total + piece
            return total

        terms = [cut(0)] + [ship(cut(d), **{axis: d}) for d in (1, 2, 3)]
    return functools.reduce(lambda a, b: a + b, terms)


def row_picks():
    lat, lon = lax.axis_index("lat"), lax.axis_index("lon")
    z, xl = lat // 2, lat % 2
    y, xh, c = lon // 4, (lon // 2) % 2, lon % 2
    x = xh * 2 + xl
    i = jnp.arange(D, dtype=jnp.int32)
    tc = (c + i // 512) % 2
    tz = (z + (i // 128) % 4) % 4
    tx = (x + (i // 32) % 4) % 4
    ty = (y + (i // 8) % 4) % 4
    block = ((tz * 2 + tx % 2) * 4 + ty) * 4 + (tx // 2) * 2 + tc
    source = block * 8 + i % 8
    return (source[:, None] == jnp.arange(D, dtype=jnp.int32)[None, :]).astype(BF16)


def window_order(a):
    a = a.reshape((2, 2, 6, 3, 12) + a.shape[3:])
    return a.transpose((1, 3, 0, 2, 4) + tuple(range(5, a.ndim)))


def per_device(latents, land_mask, norm_gain, qkv_weight, out_weight, out_cotangent):
    lon_index = lax.axis_index("lon")
    pieces = split_pieces(latents.transpose(0, 1, 3, 2))
    pieces = lax.all_to_all(pieces, "lon", split_axis=0, concat_axis=0, tiled=True)
    pick = row_picks()
    mask = jnp.roll(land_mask, -SHIFT, axis=2)
    mask = lax.dynamic_slice_in_dim(mask, lon_index * 36, 36, 2)
    mask = jnp.where(window_order(mask).reshape(TOK, 1) == 1, 0.0, -1e30).astype(F32)
    up = window_order(out_cotangent).reshape(TOK, D)
    gain = norm_gain.reshape(1, D)
    x, scaled, scaled_t = enter(pieces, gain, pick)
    att, grads, sums = [], [], []
    orders = (("dz", "dy", "dx"), ("dy", "dx", "dz"), ("dx", "dz", "dy"), ("dz", "dx", "dy"), ("dy", "dz", "dx"))
    for g in range(GROUPS):
        a, d, keep, send = attend(g, scaled, scaled_t, up, qkv_weight, out_weight, mask)
        att.append(a)
        grads.append(d)
        sums.append(scatter_sum(keep, send, orders[g]))
    back, gain_part = leave(grads, qkv_weight, x, up, gain)
    back = lax.all_to_all(back, "lon", split_axis=0, concat_axis=0, tiled=True)
    keep, send = out_weight_sum(att, up, pick)
    out_weight_grad = scatter_sum(keep, send, orders[4])
    gain_all = lax.all_to_all(gain_part.reshape(128, 8), AXES, split_axis=0, concat_axis=0, tiled=True)
    gain_grad = jnp.sum(gain_all, axis=0)
    block = block_sum(att, x, out_weight)
    block = block.reshape(2, 3, 2, 6, 12, D).transpose(2, 0, 3, 1, 4, 5).reshape(2, 12, 36, D)
    latent_grad = join_pieces(back).transpose(0, 1, 3, 2)
    qkv_weight_grad = jnp.stack(sums, axis=1).reshape(8, GROUPS, 3, GW)
    qkv_weight_grad = qkv_weight_grad.transpose(0, 2, 1, 3).reshape(8, 3 * D)
    return (block, latent_grad, qkv_weight_grad, out_weight_grad, gain_grad)


def solution(mesh):
    return jax.shard_map(
        per_device,
        mesh=mesh,
        in_specs=(
            P(None, "lat", None, "lon"),
            P(None, "lat", None),
            P(),
            P(),
            P(),
            P(None, "lat", "lon", None),
        ),
        out_specs=(
            P(None, "lat", "lon", None),
            P(None, "lat", None, "lon"),
            P(("lat", "lon"), None),
            P(("lat", "lon"), None),
            P(("lat", "lon")),
        ),
        check_vma=False,
    )
```

```python
import functools

import jax
import jax.numpy as jnp
from jax import lax
from jax.experimental import pallas as pl
from jax.experimental.pallas import tpu as pltpu
from jax.sharding import PartitionSpec as P

F32 = jnp.float32
BF16 = jnp.bfloat16
D = 1024
HEAD = 64
WIN = 144
HALF = 72
WINS = 6
TOK = WIN * WINS
SHIFT = 6
LON = 576
GROUPS = 4
ROWS = 6 * HALF + 16
GW = D // GROUPS
QUADS = GW // HEAD
SCALE = HEAD**-0.5
LOG2E = 1.4426950408889634
MIB = 1 << 20
AXES = ("lat", "lon")


def nn(a, b):
    return lax.dot_general(a, b, (((1,), (0,)), ((), ())), preferred_element_type=F32)


def nt(a, b):
    return lax.dot_general(a, b, (((1,), (1,)), ((), ())), preferred_element_type=F32)


def params(mib):
    return pltpu.CompilerParams(vmem_limit_bytes=mib * MIB)


def cost(flops, nbytes):
    return pl.CostEstimate(flops=int(flops / 10), bytes_accessed=int(nbytes / 10), transcendentals=0)


def waits(after):
    return [pl.BlockSpec(memory_space=pl.ANY)] * len(after)


def behind(kernel, count, operands, passed=0, results=1):
    def body(*refs):
        rest = refs[operands + count :]
        kernel(*refs[:operands], *rest[:results], *rest[results + passed :])

    return body


def vmem(n):
    return [pl.BlockSpec(memory_space=pltpu.VMEM)] * n


def split_kernel(z_ref, out_ref, t_ref, s_ref):
    row = lax.broadcasted_iota(jnp.int32, (LON, LON), 0)
    col = lax.broadcasted_iota(jnp.int32, (LON, LON), 1)
    source = row + SHIFT
    source = jnp.where(source >= LON, source - LON, source)
    pick = (col == source).astype(BF16)
    for r in range(12):
        both = jnp.concatenate([z_ref[0, r], z_ref[1, r]], axis=0)
        t_ref[...] = nt(pick, both)
        for v in range(48):
            at = ((r // 6) * 3 + v % 3) * HALF + (r % 6) * 12
            s_ref[v // 3, at : at + 12, :] = t_ref[12 * v : 12 * v + 12, :]
    for k in range(16):
        out_ref[k] = s_ref[k].astype(BF16)


def split_pieces(z):
    return pl.pallas_call(
        split_kernel,
        out_shape=jax.ShapeDtypeStruct((16, 6 * HALF, 128), BF16),
        in_specs=vmem(1),
        out_specs=vmem(1)[0],
        scratch_shapes=[pltpu.VMEM((LON, 128), F32), pltpu.VMEM((16, 6 * HALF, 128), F32)],
        compiler_params=params(32),
        cost_estimate=cost(2e9, 4e6),
        name="split_pieces",
    )(z)


def norm_parts(x):
    centred = x - jnp.sum(x, axis=-1, keepdims=True) * (1.0 / D)
    variance = jnp.sum(centred * centred, axis=-1, keepdims=True) * (1.0 / D)
    inv_scale = lax.rsqrt(variance + 1e-05)
    return centred * inv_scale, inv_scale


def enter_kernel(r_ref, gain_ref, pick_ref, x_ref, scaled_ref, scaled_t_ref, xs_ref):
    low = lax.broadcasted_iota(jnp.int32, (6 * HALF, 128), 1) < HEAD
    for p in range(8):
        first = r_ref[2 * p].astype(F32)
        second = r_ref[2 * p + 1].astype(F32)
        level0 = jnp.where(low, first, pltpu.roll(second, HEAD, 1))
        level1 = jnp.where(low, pltpu.roll(first, HEAD, 1), second)
        for w in range(WINS):
            at = w * WIN
            xs_ref[at : at + HALF, 128 * p : 128 * p + 128] = level0[HALF * w : HALF * w + HALF]
            xs_ref[at + HALF : at + WIN, 128 * p : 128 * p + 128] = level1[HALF * w : HALF * w + HALF]

    def rows(i, _):
        at = pl.ds(pl.multiple_of(i * 48, 48), 48)
        x = xs_ref[at, :]
        x_ref[at, :] = x.astype(BF16)
        normed, _ = norm_parts(x)
        scaled_ref[at, :] = (normed * gain_ref[...]).astype(BF16)
        return 0

    lax.fori_loop(0, TOK // 48, rows, 0)

    def turn(i, _):
        at = pl.ds(pl.multiple_of(i * 256, 256), 256)
        scaled_t_ref[at, :] = nt(pick_ref[at, :], scaled_ref[...]).astype(BF16)
        return 0

    lax.fori_loop(0, 4, turn, 0)


def enter(pieces, gain, pick):
    return pl.pallas_call(
        enter_kernel,
        out_shape=(
            jax.ShapeDtypeStruct((TOK, D), BF16),
            jax.ShapeDtypeStruct((TOK, D), BF16),
            jax.ShapeDtypeStruct((D, TOK), BF16),
        ),
        in_specs=vmem(3),
        out_specs=tuple(vmem(3)),
        scratch_shapes=[pltpu.VMEM((TOK, D), F32)],
        compiler_params=params(32),
        cost_estimate=cost(3e9, 9e6),
        name="enter",
    )(pieces, gain, pick)


def attend_kernel(
    scaled_ref, scaled_t_ref, up_ref, wq_ref, wk_ref, wv_ref, wo_ref, mask_ref,
    pick_ref, z_ref, att_ref, grad_ref, keep_ref, send_ref, q_ref, k_ref, v_ref, o_ref, other_ref,
):
    for w_ref, p_ref in ((wq_ref, q_ref), (wk_ref, k_ref), (wv_ref, v_ref)):
        p_ref[...] = nn(scaled_ref[...], w_ref[...]).astype(BF16)
    o_ref[...] = nt(up_ref[...], wo_ref[...]).astype(BF16)

    wide = (WIN, QUADS * WIN)
    key = lax.broadcasted_iota(jnp.int32, wide, 0)
    query = lax.broadcasted_iota(jnp.int32, wide, 1)
    same = query == key
    for h in range(1, QUADS):
        same = same | (query == key + h * WIN)
    other_ref[...] = jnp.where(same, 0.0, 1.0)
    lane = lax.broadcasted_iota(jnp.int32, (WIN, GW), 1)
    mine = [(lane >= HEAD * h) & (lane < HEAD * h + HEAD) for h in range(QUADS)]
    zero = jnp.zeros((WIN, GW), BF16)

    def by_head(a):
        return jnp.concatenate([jnp.where(m, a, zero) for m in mine], axis=0)

    def own_head(a):
        total = a[:WIN]
        for h in range(1, QUADS):
            total = jnp.where(mine[h], a[h * WIN : h * WIN + WIN], total)
        return total

    def window(i, _):
        at = pl.ds(pl.multiple_of(i * WIN, WIN), WIN)
        k, v = k_ref[at, :], v_ref[at, :]
        q, o = by_head(q_ref[at, :]), by_head(o_ref[at, :])
        scores = nt(k, q) * (SCALE * LOG2E) + other_ref[...] * mask_ref[at, :]
        raised = jnp.exp2(scores - jnp.max(scores, axis=0, keepdims=True))
        prob = raised * (1.0 / jnp.sum(raised, axis=0, keepdims=True))
        prob_half = prob.astype(BF16)
        prob_grad = nt(v, o)
        inner = jnp.sum(prob * prob_grad, axis=0, keepdims=True)
        score_grad = (prob * (prob_grad - inner)).astype(BF16)
        att_ref[at, :] = own_head(nn(prob_half.T, v)).astype(BF16)
        grad_ref[at, 0:GW] = (own_head(nn(score_grad.T, k)) * SCALE).astype(BF16)
        grad_ref[at, GW : 2 * GW] = (nn(score_grad, q) * SCALE).astype(BF16)
        grad_ref[at, 2 * GW : 3 * GW] = nn(prob_half, o).astype(BF16)
        return 0

    lax.fori_loop(0, WINS, window, 0)

    def weights(i, _):
        at = pl.ds(pl.multiple_of(i * 256, 256), 256)
        keep_ref[at, 0 : 3 * GW] = nn(scaled_t_ref[at, :], grad_ref[...])
        far = pl.ds(pl.multiple_of(i * 256 + 512, 256), 256)
        send_ref[at, 0 : 3 * GW] = nn(scaled_t_ref[far, :], grad_ref[...])
        return 0

    lax.fori_loop(0, 2, weights, 0)

    turned = nt(pick_ref[...], att_ref[...]).astype(BF16)
    for e in range(4):
        cols = pl.ds(pl.multiple_of((z_ref[0] ^ e) * GW, GW), GW)
        part = nn(turned, up_ref[:, cols])
        for y in range(4):
            at = 128 * y + 32 * e
            keep_ref[at : at + 32, 3 * GW :] = part[32 * y : 32 * y + 32]
            send_ref[at : at + 32, 3 * GW :] = part[128 + 32 * y : 160 + 32 * y]


def attend(g, scaled, scaled_t, up, qkv_weight, out_weight, mask, pick, z, after=()):
    full = lambda shape: pl.BlockSpec(shape, lambda i: (0, 0))
    return pl.pallas_call(
        behind(attend_kernel, len(after), 10),
        grid=(1,),
        out_shape=(
            jax.ShapeDtypeStruct((TOK, GW), BF16),
            jax.ShapeDtypeStruct((TOK, 3 * GW), BF16),
            jax.ShapeDtypeStruct((D // 2, 4 * GW), F32),
            jax.ShapeDtypeStruct((D // 2, 4 * GW), F32),
        ),
        in_specs=[
            full((TOK, D)),
            full((D, TOK)),
            full((TOK, D)),
            pl.BlockSpec((D, GW), lambda i: (0, g)),
            pl.BlockSpec((D, GW), lambda i: (0, GROUPS + g)),
            pl.BlockSpec((D, GW), lambda i: (0, 2 * GROUPS + g)),
            pl.BlockSpec((GW, D), lambda i: (g, 0)),
            full((TOK, 1)),
            full((GW, GW)),
            pl.BlockSpec(memory_space=pltpu.SMEM),
        ]
        + waits(after),
        out_specs=(
            full((TOK, GW)),
            full((TOK, 3 * GW)),
            full((D // 2, 4 * GW)),
            full((D // 2, 4 * GW)),
        ),
        scratch_shapes=[pltpu.VMEM((TOK, GW), BF16)] * 4 + [pltpu.VMEM((WIN, QUADS * WIN), F32)],
        compiler_params=params(48),
        cost_estimate=cost(8e9, 15e6),
        name="attend",
    )(scaled, scaled_t, up, qkv_weight, qkv_weight, qkv_weight, out_weight, mask, pick, z, *after)


def block_kernel(a0, a1, a2, a3, x_ref, w_ref, out_ref):
    def rows(i, _):
        at = pl.ds(pl.multiple_of(i * 432, 432), 432)
        total = x_ref[at, :].astype(F32)
        for g, a in enumerate((a0, a1, a2, a3)):
            total = total + nn(a[at, :], w_ref[GW * g : GW * g + GW, :])
        out_ref[at, :] = total.astype(BF16)
        return 0

    lax.fori_loop(0, 2, rows, 0)


def block_sum(att, x, out_weight, passed, after):
    after = tuple(passed) + tuple(after)
    return pl.pallas_call(
        behind(block_kernel, len(after), 6, len(passed)),
        out_shape=(jax.ShapeDtypeStruct((TOK, D), BF16),)
        + tuple(jax.ShapeDtypeStruct(p.shape, p.dtype) for p in passed),
        in_specs=vmem(6) + waits(after),
        out_specs=tuple(vmem(1) + waits(passed)),
        input_output_aliases={6 + i: 1 + i for i in range(len(passed))},
        compiler_params=params(32),
        cost_estimate=cost(2e9, 8e6),
        name="block_sum",
    )(*att, x, out_weight, *after)


def product_kernel(g0, g1, g2, g3, w_ref, n_ref):
    def product(i, _):
        at = pl.ds(pl.multiple_of(i * 432, 432), 432)
        total = None
        for g, d in enumerate((g0, g1, g2, g3)):
            for part in range(3):
                base = part * D + g * GW
                piece = nt(d[at, part * GW : part * GW + GW], w_ref[:, base : base + GW])
                total = piece if total is None else total + piece
        n_ref[at, :] = total
        return 0

    lax.fori_loop(0, 2, product, 0)


def product(grads, qkv_weight, after=()):
    return pl.pallas_call(
        behind(product_kernel, len(after), 5),
        out_shape=jax.ShapeDtypeStruct((TOK, D), F32),
        in_specs=vmem(5) + waits(after),
        out_specs=vmem(1)[0],
        compiler_params=params(40),
        cost_estimate=cost(6e9, 15e6),
        name="product",
    )(*grads, qkv_weight, *after)


def leave_kernel(s_ref, x_ref, up_ref, gain_ref, mix_ref, out_ref, n_ref):
    def rows(i, gain_sum):
        at = pl.ds(pl.multiple_of(i * 48, 48), 48)
        normed, inv_scale = norm_parts(x_ref[at, :].astype(F32))
        n = s_ref[at, :]
        both = n * normed
        gain = gain_ref[...]
        g = n * gain
        mean_g = jnp.sum(g, axis=-1, keepdims=True) * (1.0 / D)
        mean_gn = jnp.sum(both * gain, axis=-1, keepdims=True) * (1.0 / D)
        n_ref[at, :] = up_ref[at, :].astype(F32) + inv_scale * (g - mean_g - normed * mean_gn)
        return gain_sum + jnp.sum(both.reshape(6, 8, D), axis=0)

    gain_sum = lax.fori_loop(0, TOK // 48, rows, jnp.zeros((8, D), F32))
    whole = jnp.sum(gain_sum, axis=0, keepdims=True)
    high = whole.astype(BF16).astype(F32)
    mid = (whole - high).astype(BF16).astype(F32)
    row16 = lax.broadcasted_iota(jnp.int32, (16, D), 0)
    split = jnp.where(row16 == 0, high, jnp.where(row16 == 1, mid, whole - high - mid))
    split = jnp.where(row16 < 3, split, 0.0).astype(BF16)
    split = nn(split, mix_ref[...]).astype(BF16)

    low = lax.broadcasted_iota(jnp.int32, (6 * HALF, 128), 1) < HEAD
    for p in range(8):
        cols = slice(128 * p, 128 * p + 128)
        level0 = jnp.concatenate([n_ref[WIN * w : WIN * w + HALF, cols] for w in range(WINS)], axis=0)
        level1 = jnp.concatenate([n_ref[WIN * w + HALF : WIN * w + WIN, cols] for w in range(WINS)], axis=0)
        out_ref[2 * p, 0 : 6 * HALF] = jnp.where(low, level0, pltpu.roll(level1, HEAD, 1)).astype(BF16)
        out_ref[2 * p + 1, 0 : 6 * HALF] = jnp.where(low, pltpu.roll(level0, HEAD, 1), level1).astype(BF16)
        out_ref[2 * p, 6 * HALF :] = split[:, cols]
        out_ref[2 * p + 1, 6 * HALF :] = split[:, cols]


def leave(norm_grad, x, up, gain, mix, after=()):
    return pl.pallas_call(
        behind(leave_kernel, len(after), 5),
        out_shape=jax.ShapeDtypeStruct((16, ROWS, 128), BF16),
        in_specs=vmem(5) + waits(after),
        out_specs=vmem(1)[0],
        scratch_shapes=[pltpu.VMEM((TOK, D), F32)],
        compiler_params=params(32),
        cost_estimate=cost(4e9, 10e6),
        name="leave",
    )(norm_grad, x, up, gain, mix, *after)


def join_kernel(r_ref, out_ref, gain_ref, s_ref, t_ref):
    gain = None
    for k in range(16):
        s_ref[k] = r_ref[k, 0 : 6 * HALF].astype(F32)
        term = r_ref[k, 6 * HALF :].astype(F32)
        gain = term if gain is None else gain + term
    gain_ref[...] = jnp.sum(gain, axis=0, keepdims=True)
    same = lax.broadcasted_iota(jnp.int32, (128, 128), 0) == lax.broadcasted_iota(
        jnp.int32, (128, 128), 1
    )
    same = same.astype(BF16)
    for r in range(12):
        for v in range(48):
            at = ((r // 6) * 3 + v % 3) * HALF + (r % 6) * 12
            to = 12 * v + SHIFT
            if to + 12 <= LON:
                t_ref[to : to + 12, :] = s_ref[v // 3, at : at + 12, :]
            else:
                t_ref[to:LON, :] = s_ref[v // 3, at : at + LON - to, :]
                t_ref[0 : to + 12 - LON, :] = s_ref[v // 3, at + LON - to : at + 12, :]
        turned = nt(same, t_ref[...].astype(BF16)).astype(BF16)
        out_ref[0, r] = turned[:HEAD]
        out_ref[1, r] = turned[HEAD:]


def join_pieces(pieces, passed, after):
    after = tuple(passed) + tuple(after)
    return pl.pallas_call(
        behind(join_kernel, len(after), 1, len(passed), 2),
        out_shape=(
            jax.ShapeDtypeStruct((2, 12, HEAD, LON), BF16),
            jax.ShapeDtypeStruct((1, 128), F32),
        )
        + tuple(jax.ShapeDtypeStruct(p.shape, p.dtype) for p in passed),
        in_specs=vmem(1) + waits(after),
        out_specs=tuple(vmem(2) + waits(passed)),
        input_output_aliases={1 + i: 2 + i for i in range(len(passed))},
        scratch_shapes=[pltpu.VMEM((16, 6 * HALF, 128), F32), pltpu.VMEM((LON, 128), F32)],
        compiler_params=params(32),
        cost_estimate=cost(2e9, 4e6),
        name="join_pieces",
    )(pieces, *after)


def device_index(x, y, z, core):
    return ((z * 2 + x % 2) * 4 + y) * 4 + (x // 2) * 2 + core


def swapped(z=0, x=0, y=0, core=0):
    pairs = []
    for px in range(4):
        for py in range(4):
            for pz in range(4):
                for c in range(2):
                    to = device_index(px ^ x, py ^ y, pz ^ z, c ^ core)
                    pairs.append((device_index(px, py, pz, c), to))
    return sorted(pairs)


class Sum:
    def __init__(self, keep, got):
        self.tail = (8, keep.shape[-1])
        self.spots = {n: (0, 1, 2, 3) for n in "yzx"}
        self.whole = {n: {e: e for e in range(4)} for n in "yzx"}
        self.terms = [(keep.reshape((4, 4, 4) + self.tail), self.whole, 0)]
        self.terms.append((got.reshape((4, 4, 4) + self.tail), self.whole, 0))

    def columns(self, low, high):
        part = Sum.__new__(Sum)
        part.tail, part.whole, part.spots = (8, high - low), self.whole, dict(self.spots)
        part.terms = [(a, places, low) for a, places, _ in self.terms]
        return part

    def cut(self, name, chosen):
        total = None
        spots = dict(self.spots)
        spots[name] = chosen
        for array, places, low in self.terms:
            index = tuple(
                slice(places[n][spots[n][0]], places[n][spots[n][-1]] + 1) for n in "yzx"
            )
            piece = array[index + (slice(None), slice(low, low + self.tail[1]))]
            total = piece if total is None else total + piece
        return total

    def offer(self, name, by):
        if len(self.spots[name]) == 4:
            give, rest = ((1, 2), (0, 3)) if by == 1 else ((2, 3), (0, 1))
        else:
            give, rest = (by,), (0,)
        piece = self.cut(name, give)
        self.spots[name] = rest
        places = {n: {e: i for i, e in enumerate(self.spots[n])} for n in "yzx"}
        places[name] = {e ^ by: i for i, e in enumerate(give)}
        return piece, places

    def ring_y(self, y):
        (keep, _, _), (got, _, _) = self.terms
        total = ordered_sum(keep, got, y)
        rest = total.reshape(4 * 128, self.tail[1])
        rest = lax.psum_scatter(rest, "lon", scatter_dimension=0, axis_index_groups=Y_RINGS, tiled=True)
        self.reduced = rest
        self.spots["y"] = (0,)
        places = dict(self.whole)
        places["y"] = {0: 0}
        self.terms = [(rest.reshape((1, 4, 4) + self.tail), places, 0)]
        return total

    def cells(self):
        found = []
        for array, places, low in self.terms:
            at = places["y"][0] * array.shape[1] + places["z"][0]
            found.append((array.reshape(-1, 32, array.shape[-1]), at, low // self.tail[1]))
        return found


Y_RINGS = [[c, c + 4, c + 8, c + 12] for c in range(4)]


def exchange(sums, name, by):
    offers = [s.offer(name, by) for s in sums]
    flat = [piece.reshape((-1,) + piece.shape[3:]) for piece, _ in offers]
    out = flat[0] if len(flat) == 1 else jnp.concatenate(flat, axis=-1)
    got = lax.ppermute(out, AXES, swapped(**{name: by}))
    at = 0
    for s, (piece, places) in zip(sums, offers):
        wide = piece.shape[-1]
        s.terms.append((got.reshape(piece.shape[:3] + (8, -1)), places, at))
        at += wide
    return out, got


def add_kernel(y_ref, a_ref, b_ref, out_ref):
    out_ref[...] = a_ref[...] + b_ref[...]


def ordered_sum(a, b, y):
    a, b = (t.reshape(4, 128, t.shape[-1]) for t in (a, b))
    block = (1,) + a.shape[1:]
    return pl.pallas_call(
        add_kernel,
        grid_spec=pltpu.PrefetchScalarGridSpec(
            num_scalar_prefetch=1,
            grid=(4,),
            in_specs=[pl.BlockSpec(block, lambda i, y: (i ^ y[0], 0, 0))] * 2,
            out_specs=pl.BlockSpec(block, lambda i, y: (i, 0, 0)),
        ),
        out_shape=jax.ShapeDtypeStruct(a.shape, F32),
        compiler_params=params(16),
        cost_estimate=cost(0, 5e6),
        name="ordered_sum",
    )(y, a, b)


def last_cut_kernel(counts, *refs):
    ins, gain_ref, outs = refs[: sum(counts)], refs[sum(counts)], refs[sum(counts) + 1 :]
    at, col = 0, 0
    for n in counts:
        total = ins[at][0]
        for r in ins[at + 1 : at + n]:
            total = total + r[0]
        wide = total.shape[-1]
        for e in range(4):
            outs[e][:, col : col + wide] = total[8 * e : 8 * e + 8]
        at, col = at + n, col + wide
    row = lax.broadcasted_iota(jnp.int32, (8, 128), 0)
    outs[1][:, col:] = jnp.where(row == 0, gain_ref[...], 0.0)


def last_cut(parts, gain):
    cells = [t.cells() for t in parts]
    counts = tuple(len(c) for c in cells)
    widths = [t.tail[1] for t, c in zip(parts, cells) for _ in c]
    cells = sum(cells, [])
    whole = lambda shape: pl.BlockSpec(shape, lambda i: (0, 0))
    wide = [4 * D, 4 * D + 128, 4 * D, 4 * D]
    return pl.pallas_call(
        functools.partial(last_cut_kernel, counts),
        grid=(1,),
        in_specs=[
            pl.BlockSpec((1, 32, wide), functools.partial(lambda at, col, i: (at, 0, col), at, col))
            for (_, at, col), wide in zip(cells, widths)
        ]
        + [whole((1, 128))],
        out_specs=tuple(whole((8, w)) for w in wide),
        out_shape=tuple(jax.ShapeDtypeStruct((8, w), F32) for w in wide),
        compiler_params=params(24),
        cost_estimate=cost(0, 5e6),
        name="last_cut",
    )(*[a for a, _, _ in cells], gain)


def quarter_kernel(own, got1, got2, got3, gain_ref, z_ref, out_ref, s0, s1, s2, s3, q_ref):
    total = own[...] + got1[:, : 4 * D] + got2[...] + got3[...]
    for g in range(GROUPS):
        for part in range(3):
            at = part * D + g * GW
            out_ref[:, at : at + GW] = total[:, g * D + part * GW : g * D + part * GW + GW]
        q_ref[g] = total[:, g * D + 3 * GW : g * D + D]
    gain = jnp.broadcast_to(gain_ref[...] + got1[0:1, 4 * D :], (8, 128))
    for d, send in enumerate((s0, s1, s2, s3)):
        send[:, :GW] = q_ref[z_ref[0] ^ d]
        send[:, GW:] = gain


def quarters_of(own, got, gain, z):
    return pl.pallas_call(
        quarter_kernel,
        out_shape=(jax.ShapeDtypeStruct((8, 3 * D), F32),)
        + (jax.ShapeDtypeStruct((8, GW + 128), F32),) * 4,
        in_specs=vmem(5) + [pl.BlockSpec(memory_space=pltpu.SMEM)],
        out_specs=tuple(vmem(5)),
        scratch_shapes=[pltpu.VMEM((4, 8, GW), F32)],
        compiler_params=params(16),
        cost_estimate=cost(0, 1e6),
        name="quarters_of",
    )(own, *got, gain, z)


def gather_kernel(m0, m1, m2, m3, z_ref, out_ref, gain_ref, q_ref):
    gain = None
    for d, m in enumerate((m0, m1, m2, m3)):
        q_ref[d] = m[:, :GW]
        term = m[0:1, GW:]
        gain = term if gain is None else gain + term
    for e in range(4):
        out_ref[:, e * GW : e * GW + GW] = q_ref[z_ref[0] ^ e]
    gain_ref[...] = gain


def gather_quarters(pieces, z):
    return pl.pallas_call(
        gather_kernel,
        out_shape=(jax.ShapeDtypeStruct((8, D), F32), jax.ShapeDtypeStruct((1, 128), F32)),
        in_specs=vmem(4) + [pl.BlockSpec(memory_space=pltpu.SMEM)],
        out_specs=tuple(vmem(2)),
        scratch_shapes=[pltpu.VMEM((4, 8, GW), F32)],
        compiler_params=params(16),
        cost_estimate=cost(0, 1e6),
        name="gather_quarters",
    )(*pieces, z)


def row_picks():
    lat, lon = lax.axis_index("lat"), lax.axis_index("lon")
    z, xl = lat // 2, lat % 2
    y, xh, c = lon // 4, (lon // 2) % 2, lon % 2
    x = xh * 2 + xl
    i = jnp.arange(D, dtype=jnp.int32)
    tc = c ^ (i // 512)
    ty = y ^ ((i // 128) % 4)
    tz = z ^ ((i // 32) % 4)
    tx = x ^ ((i // 8) % 4)
    block = ((tz * 2 + tx % 2) * 4 + ty) * 4 + (tx // 2) * 2 + tc
    source = block * 8 + i % 8
    i = jnp.arange(GW, dtype=jnp.int32)
    tc = c ^ (i // 128)
    ty = y ^ ((i // 32) % 4)
    tx = x ^ ((i // 8) % 4)
    block = ((tx % 2) * 4 + ty) * 4 + (tx // 2) * 2 + tc
    group = block * 8 + i % 8
    return tuple(
        (t[:, None] == jnp.arange(t.shape[0], dtype=jnp.int32)[None, :]).astype(BF16)
        for t in (source, group)
    )


def gain_mix():
    i = jnp.arange(D, dtype=jnp.int32)
    source = ((i // 8) % 8) * 128 + (i // 64) * 8 + i % 8
    return (jnp.arange(D, dtype=jnp.int32)[:, None] == source[None, :]).astype(BF16)


def window_order(a):
    a = a.reshape((2, 2, 6, 3, 12) + a.shape[3:])
    return a.transpose((1, 3, 0, 2, 4) + tuple(range(5, a.ndim)))


def per_device(latents, land_mask, norm_gain, qkv_weight, out_weight, out_cotangent):
    lon_index = lax.axis_index("lon")
    pieces = split_pieces(latents.transpose(0, 1, 3, 2))
    pieces = lax.all_to_all(pieces, "lon", split_axis=0, concat_axis=0, tiled=True)
    pick, pick_group = row_picks()
    z_index = (lax.axis_index("lat") // 2).reshape(1)
    mask = jnp.roll(land_mask, -SHIFT, axis=2)
    mask = lax.dynamic_slice_in_dim(mask, lon_index * 36, 36, 2)
    mask = jnp.where(window_order(mask).reshape(TOK, 1) == 1, 0.0, -1e30).astype(F32)
    up = window_order(out_cotangent).reshape(TOK, D)
    gain = norm_gain.reshape(1, D)
    x, scaled, scaled_t = enter(pieces, gain, pick)
    y_index = (lon_index // 4).reshape(1)
    att, grads = [], []

    def heads(g, after):
        a, d, keep, send = attend(
            g, scaled, scaled_t, up, qkv_weight, out_weight, mask, pick_group, z_index, after
        )
        att.append(a)
        grads.append(d)
        return Sum(keep, lax.ppermute(send, AXES, swapped(core=1)))

    def newest(t):
        return t.terms[-1][0]

    s0 = heads(0, ())
    s1 = heads(1, ())
    total = s0.ring_y(y_index)
    s2 = heads(2, (total,))
    total = s1.ring_y(y_index)
    s3 = heads(3, (total,))
    out2, _ = exchange([s2], "z", 1)
    norm_grad = product(grads, qkv_weight, (out2,))
    s3, s4 = s3.columns(0, 2 * GW), s3.columns(2 * GW, 4 * GW)
    out3, _ = exchange([s3], "z", 1)
    out4, _ = exchange([s4], "z", 3)
    leaving = leave(norm_grad, x, up, gain, gain_mix(), (out3, out4))
    back = lax.all_to_all(leaving, "lon", split_axis=0, concat_axis=0, tiled=True)
    def hand(sums, arrays):
        for t, p in zip(sums, arrays):
            t.terms[-1] = (p,) + t.terms[-1][1:]

    waiting = (s2, s3, s4)
    block, *passed = block_sum(att, x, out_weight, [newest(t) for t in waiting], (leaving,))
    hand(waiting, passed)
    exchange([s2], "z", 3)
    exchange([s3], "z", 3)
    exchange([s4], "z", 1)
    exchange([s2, s3, s4], "y", 1)
    exchange([s0, s1], "z", 1)
    joined, gain_sum, one, two = join_pieces(back, (newest(s2), newest(s0)), (block,))
    hand((s2, s3, s4, s0, s1), (one, one, one, two, two))
    exchange([s2, s3, s4], "y", 3)
    exchange([s0, s1], "z", 3)
    own, *send = last_cut((s0, s1, s2, s3, s4), gain_sum)
    got = [lax.ppermute(a, AXES, swapped(x=d)) for d, a in zip((1, 2, 3), send)]
    qkv_weight_grad, own, *send = quarters_of(own, got, gain_sum, z_index)
    got = [lax.ppermute(a, AXES, swapped(z=d)) for d, a in zip((1, 2, 3), send)]
    out_weight_grad, gain_sum = gather_quarters([own] + got, z_index)
    at = (lon_index % 2) * 64 + lax.axis_index("lat") * 8
    gain_grad = lax.dynamic_slice_in_dim(gain_sum.reshape(128), at, 8, 0)
    block = block.reshape(2, 3, 2, 6, 12, D).transpose(2, 0, 3, 1, 4, 5).reshape(2, 12, 36, D)
    latent_grad = joined.transpose(0, 1, 3, 2)
    return (block, latent_grad, qkv_weight_grad, out_weight_grad, gain_grad)


def solution(mesh):
    return jax.shard_map(
        per_device,
        mesh=mesh,
        in_specs=(
            P(None, "lat", None, "lon"),
            P(None, "lat", None),
            P(),
            P(),
            P(),
            P(None, "lat", "lon", None),
        ),
        out_specs=(
            P(None, "lat", "lon", None),
            P(None, "lat", None, "lon"),
            P(("lat", "lon"), None),
            P(("lat", "lon"), None),
            P(("lat", "lon")),
        ),
        check_vma=False,
    )
```

```python
import functools

import jax
import jax.numpy as jnp
from jax import lax
from jax.experimental import pallas as pl
from jax.experimental.pallas import tpu as pltpu
from jax.sharding import PartitionSpec as P

F32 = jnp.float32
BF16 = jnp.bfloat16
D = 1024
HEAD = 64
WIN = 144
HALF = 72
WINS = 6
TOK = WIN * WINS
SHIFT = 6
LON = 576
GROUPS = 4
ROWS = 6 * HALF + 16
GW = D // GROUPS
QUADS = GW // HEAD
SCALE = HEAD**-0.5
LOG2E = 1.4426950408889634
MIB = 1 << 20
AXES = ("lat", "lon")


def nn(a, b):
    return lax.dot_general(a, b, (((1,), (0,)), ((), ())), preferred_element_type=F32)


def nt(a, b):
    return lax.dot_general(a, b, (((1,), (1,)), ((), ())), preferred_element_type=F32)


def params(mib):
    return pltpu.CompilerParams(vmem_limit_bytes=mib * MIB)


def cost(flops, nbytes):
    return pl.CostEstimate(flops=int(flops / 10), bytes_accessed=int(nbytes / 10), transcendentals=0)


def waits(after):
    return [pl.BlockSpec(memory_space=pl.ANY)] * len(after)


def behind(kernel, count, operands, passed=0, results=1):
    def body(*refs):
        rest = refs[operands + count :]
        kernel(*refs[:operands], *rest[:results], *rest[results + passed :])

    return body


def vmem(n):
    return [pl.BlockSpec(memory_space=pltpu.VMEM)] * n


def split_kernel(z_ref, out_ref, t_ref, s_ref):
    row = lax.broadcasted_iota(jnp.int32, (LON, LON), 0)
    col = lax.broadcasted_iota(jnp.int32, (LON, LON), 1)
    source = row + SHIFT
    source = jnp.where(source >= LON, source - LON, source)
    pick = (col == source).astype(BF16)
    for r in range(12):
        both = jnp.concatenate([z_ref[0, r], z_ref[1, r]], axis=0)
        t_ref[...] = nt(pick, both)
        for v in range(48):
            at = ((r // 6) * 3 + v % 3) * HALF + (r % 6) * 12
            s_ref[v // 3, at : at + 12, :] = t_ref[12 * v : 12 * v + 12, :]
    for k in range(16):
        out_ref[k] = s_ref[k].astype(BF16)


def split_pieces(z):
    return pl.pallas_call(
        split_kernel,
        out_shape=jax.ShapeDtypeStruct((16, 6 * HALF, 128), BF16),
        in_specs=vmem(1),
        out_specs=vmem(1)[0],
        scratch_shapes=[pltpu.VMEM((LON, 128), F32), pltpu.VMEM((16, 6 * HALF, 128), F32)],
        compiler_params=params(32),
        cost_estimate=cost(2e9, 4e6),
        name="split_pieces",
    )(z)


def norm_parts(x):
    centred = x - jnp.sum(x, axis=-1, keepdims=True) * (1.0 / D)
    variance = jnp.sum(centred * centred, axis=-1, keepdims=True) * (1.0 / D)
    inv_scale = lax.rsqrt(variance + 1e-05)
    return centred * inv_scale, inv_scale


def enter_kernel(r_ref, gain_ref, pick_ref, x_ref, scaled_ref, scaled_t_ref, xs_ref):
    low = lax.broadcasted_iota(jnp.int32, (6 * HALF, 128), 1) < HEAD
    for p in range(8):
        first = r_ref[2 * p].astype(F32)
        second = r_ref[2 * p + 1].astype(F32)
        level0 = jnp.where(low, first, pltpu.roll(second, HEAD, 1))
        level1 = jnp.where(low, pltpu.roll(first, HEAD, 1), second)
        for w in range(WINS):
            at = w * WIN
            xs_ref[at : at + HALF, 128 * p : 128 * p + 128] = level0[HALF * w : HALF * w + HALF]
            xs_ref[at + HALF : at + WIN, 128 * p : 128 * p + 128] = level1[HALF * w : HALF * w + HALF]

    def rows(i, _):
        at = pl.ds(pl.multiple_of(i * 48, 48), 48)
        x = xs_ref[at, :]
        x_ref[at, :] = x.astype(BF16)
        normed, _ = norm_parts(x)
        scaled_ref[at, :] = (normed * gain_ref[...]).astype(BF16)
        return 0

    lax.fori_loop(0, TOK // 48, rows, 0)

    def turn(i, _):
        at = pl.ds(pl.multiple_of(i * 256, 256), 256)
        scaled_t_ref[at, :] = nt(pick_ref[at, :], scaled_ref[...]).astype(BF16)
        return 0

    lax.fori_loop(0, 4, turn, 0)


def enter(pieces, gain, pick):
    return pl.pallas_call(
        enter_kernel,
        out_shape=(
            jax.ShapeDtypeStruct((TOK, D), BF16),
            jax.ShapeDtypeStruct((TOK, D), BF16),
            jax.ShapeDtypeStruct((D, TOK), BF16),
        ),
        in_specs=vmem(3),
        out_specs=tuple(vmem(3)),
        scratch_shapes=[pltpu.VMEM((TOK, D), F32)],
        compiler_params=params(32),
        cost_estimate=cost(3e9, 9e6),
        name="enter",
    )(pieces, gain, pick)


def attend_kernel(
    scaled_ref, scaled_t_ref, up_ref, wq_ref, wk_ref, wv_ref, wo_ref, mask_ref,
    pick_ref, z_ref, att_ref, grad_ref, keep_ref, send_ref, q_ref, k_ref, v_ref, o_ref, other_ref,
):
    for w_ref, p_ref in ((wq_ref, q_ref), (wk_ref, k_ref), (wv_ref, v_ref)):
        p_ref[...] = nn(scaled_ref[...], w_ref[...]).astype(BF16)
    o_ref[...] = nt(up_ref[...], wo_ref[...]).astype(BF16)

    wide = (WIN, QUADS * WIN)
    key = lax.broadcasted_iota(jnp.int32, wide, 0)
    query = lax.broadcasted_iota(jnp.int32, wide, 1)
    same = query == key
    for h in range(1, QUADS):
        same = same | (query == key + h * WIN)
    other_ref[...] = jnp.where(same, 0.0, 1.0)
    lane = lax.broadcasted_iota(jnp.int32, (WIN, GW), 1)
    mine = [(lane >= HEAD * h) & (lane < HEAD * h + HEAD) for h in range(QUADS)]
    zero = jnp.zeros((WIN, GW), BF16)

    def by_head(a):
        return jnp.concatenate([jnp.where(m, a, zero) for m in mine], axis=0)

    def own_head(a):
        total = a[:WIN]
        for h in range(1, QUADS):
            total = jnp.where(mine[h], a[h * WIN : h * WIN + WIN], total)
        return total

    def window(i, _):
        at = pl.ds(pl.multiple_of(i * WIN, WIN), WIN)
        k, v = k_ref[at, :], v_ref[at, :]
        q, o = by_head(q_ref[at, :]), by_head(o_ref[at, :])
        scores = nt(k, q) * (SCALE * LOG2E) + other_ref[...] * mask_ref[at, :]
        raised = jnp.exp2(scores - jnp.max(scores, axis=0, keepdims=True))
        prob = raised * (1.0 / jnp.sum(raised, axis=0, keepdims=True))
        prob_half = prob.astype(BF16)
        prob_grad = nt(v, o)
        inner = jnp.sum(prob * prob_grad, axis=0, keepdims=True)
        score_grad = (prob * (prob_grad - inner)).astype(BF16)
        att_ref[at, :] = own_head(nn(prob_half.T, v)).astype(BF16)
        grad_ref[at, 0:GW] = (own_head(nn(score_grad.T, k)) * SCALE).astype(BF16)
        grad_ref[at, GW : 2 * GW] = (nn(score_grad, q) * SCALE).astype(BF16)
        grad_ref[at, 2 * GW : 3 * GW] = nn(prob_half, o).astype(BF16)
        return 0

    lax.fori_loop(0, WINS, window, 0)

    def weights(i, _):
        at = pl.ds(pl.multiple_of(i * 256, 256), 256)
        keep_ref[at, 0 : 3 * GW] = nn(scaled_t_ref[at, :], grad_ref[...])
        far = pl.ds(pl.multiple_of(i * 256 + 512, 256), 256)
        send_ref[at, 0 : 3 * GW] = nn(scaled_t_ref[far, :], grad_ref[...])
        return 0

    lax.fori_loop(0, 2, weights, 0)

    turned = nt(pick_ref[...], att_ref[...]).astype(BF16)
    for e in range(4):
        cols = pl.ds(pl.multiple_of((z_ref[0] ^ e) * GW, GW), GW)
        part = nn(turned, up_ref[:, cols])
        for y in range(4):
            at = 128 * y + 32 * e
            keep_ref[at : at + 32, 3 * GW :] = part[32 * y : 32 * y + 32]
            send_ref[at : at + 32, 3 * GW :] = part[128 + 32 * y : 160 + 32 * y]


def attend(g, scaled, scaled_t, up, qkv_weight, out_weight, mask, pick, z, after=()):
    full = lambda shape: pl.BlockSpec(shape, lambda i: (0, 0))
    return pl.pallas_call(
        behind(attend_kernel, len(after), 10),
        grid=(1,),
        out_shape=(
            jax.ShapeDtypeStruct((TOK, GW), BF16),
            jax.ShapeDtypeStruct((TOK, 3 * GW), BF16),
            jax.ShapeDtypeStruct((D // 2, 4 * GW), F32),
            jax.ShapeDtypeStruct((D // 2, 4 * GW), F32),
        ),
        in_specs=[
            full((TOK, D)),
            full((D, TOK)),
            full((TOK, D)),
            pl.BlockSpec((D, GW), lambda i: (0, g)),
            pl.BlockSpec((D, GW), lambda i: (0, GROUPS + g)),
            pl.BlockSpec((D, GW), lambda i: (0, 2 * GROUPS + g)),
            pl.BlockSpec((GW, D), lambda i: (g, 0)),
            full((TOK, 1)),
            full((GW, GW)),
            pl.BlockSpec(memory_space=pltpu.SMEM),
        ]
        + waits(after),
        out_specs=(
            full((TOK, GW)),
            full((TOK, 3 * GW)),
            full((D // 2, 4 * GW)),
            full((D // 2, 4 * GW)),
        ),
        scratch_shapes=[pltpu.VMEM((TOK, GW), BF16)] * 4 + [pltpu.VMEM((WIN, QUADS * WIN), F32)],
        compiler_params=params(48),
        cost_estimate=cost(8e9, 15e6),
        name="attend",
    )(scaled, scaled_t, up, qkv_weight, qkv_weight, qkv_weight, out_weight, mask, pick, z, *after)


def block_kernel(a0, a1, a2, a3, x_ref, w_ref, out_ref):
    def rows(i, _):
        at = pl.ds(pl.multiple_of(i * 432, 432), 432)
        total = x_ref[at, :].astype(F32)
        for g, a in enumerate((a0, a1, a2, a3)):
            total = total + nn(a[at, :], w_ref[GW * g : GW * g + GW, :])
        out_ref[at, :] = total.astype(BF16)
        return 0

    lax.fori_loop(0, 2, rows, 0)


def block_sum(att, x, out_weight, passed, after):
    after = tuple(passed) + tuple(after)
    return pl.pallas_call(
        behind(block_kernel, len(after), 6, len(passed)),
        out_shape=(jax.ShapeDtypeStruct((TOK, D), BF16),)
        + tuple(jax.ShapeDtypeStruct(p.shape, p.dtype) for p in passed),
        in_specs=vmem(6) + waits(after),
        out_specs=tuple(vmem(1) + waits(passed)),
        input_output_aliases={6 + i: 1 + i for i in range(len(passed))},
        compiler_params=params(32),
        cost_estimate=cost(2e9, 8e6),
        name="block_sum",
    )(*att, x, out_weight, *after)


def product_kernel(g0, g1, g2, g3, w_ref, n_ref):
    def product(i, _):
        at = pl.ds(pl.multiple_of(i * 432, 432), 432)
        total = None
        for g, d in enumerate((g0, g1, g2, g3)):
            for part in range(3):
                base = part * D + g * GW
                piece = nt(d[at, part * GW : part * GW + GW], w_ref[:, base : base + GW])
                total = piece if total is None else total + piece
        n_ref[at, :] = total
        return 0

    lax.fori_loop(0, 2, product, 0)


def product(grads, qkv_weight, after=()):
    return pl.pallas_call(
        behind(product_kernel, len(after), 5),
        out_shape=jax.ShapeDtypeStruct((TOK, D), F32),
        in_specs=vmem(5) + waits(after),
        out_specs=vmem(1)[0],
        compiler_params=params(40),
        cost_estimate=cost(6e9, 15e6),
        name="product",
    )(*grads, qkv_weight, *after)


def leave_kernel(s_ref, x_ref, up_ref, gain_ref, mix_ref, out_ref, n_ref):
    def rows(i, gain_sum):
        at = pl.ds(pl.multiple_of(i * 48, 48), 48)
        normed, inv_scale = norm_parts(x_ref[at, :].astype(F32))
        n = s_ref[at, :]
        both = n * normed
        gain = gain_ref[...]
        g = n * gain
        mean_g = jnp.sum(g, axis=-1, keepdims=True) * (1.0 / D)
        mean_gn = jnp.sum(both * gain, axis=-1, keepdims=True) * (1.0 / D)
        n_ref[at, :] = up_ref[at, :].astype(F32) + inv_scale * (g - mean_g - normed * mean_gn)
        return gain_sum + jnp.sum(both.reshape(6, 8, D), axis=0)

    gain_sum = lax.fori_loop(0, TOK // 48, rows, jnp.zeros((8, D), F32))
    whole = jnp.sum(gain_sum, axis=0, keepdims=True)
    high = whole.astype(BF16).astype(F32)
    mid = (whole - high).astype(BF16).astype(F32)
    row16 = lax.broadcasted_iota(jnp.int32, (16, D), 0)
    split = jnp.where(row16 == 0, high, jnp.where(row16 == 1, mid, whole - high - mid))
    split = jnp.where(row16 < 3, split, 0.0).astype(BF16)
    split = nn(split, mix_ref[...]).astype(BF16)

    low = lax.broadcasted_iota(jnp.int32, (6 * HALF, 128), 1) < HEAD
    for p in range(8):
        cols = slice(128 * p, 128 * p + 128)
        level0 = jnp.concatenate([n_ref[WIN * w : WIN * w + HALF, cols] for w in range(WINS)], axis=0)
        level1 = jnp.concatenate([n_ref[WIN * w + HALF : WIN * w + WIN, cols] for w in range(WINS)], axis=0)
        out_ref[2 * p, 0 : 6 * HALF] = jnp.where(low, level0, pltpu.roll(level1, HEAD, 1)).astype(BF16)
        out_ref[2 * p + 1, 0 : 6 * HALF] = jnp.where(low, pltpu.roll(level0, HEAD, 1), level1).astype(BF16)
        out_ref[2 * p, 6 * HALF :] = split[:, cols]
        out_ref[2 * p + 1, 6 * HALF :] = split[:, cols]


def leave(norm_grad, x, up, gain, mix, after=()):
    return pl.pallas_call(
        behind(leave_kernel, len(after), 5),
        out_shape=jax.ShapeDtypeStruct((16, ROWS, 128), BF16),
        in_specs=vmem(5) + waits(after),
        out_specs=vmem(1)[0],
        scratch_shapes=[pltpu.VMEM((TOK, D), F32)],
        compiler_params=params(32),
        cost_estimate=cost(4e9, 10e6),
        name="leave",
    )(norm_grad, x, up, gain, mix, *after)


def join_kernel(r_ref, out_ref, gain_ref, s_ref, t_ref):
    gain = None
    for k in range(16):
        s_ref[k] = r_ref[k, 0 : 6 * HALF].astype(F32)
        term = r_ref[k, 6 * HALF :].astype(F32)
        gain = term if gain is None else gain + term
    gain_ref[...] = jnp.sum(gain, axis=0, keepdims=True)
    same = lax.broadcasted_iota(jnp.int32, (128, 128), 0) == lax.broadcasted_iota(
        jnp.int32, (128, 128), 1
    )
    same = same.astype(BF16)
    for r in range(12):
        for v in range(48):
            at = ((r // 6) * 3 + v % 3) * HALF + (r % 6) * 12
            to = 12 * v + SHIFT
            if to + 12 <= LON:
                t_ref[to : to + 12, :] = s_ref[v // 3, at : at + 12, :]
            else:
                t_ref[to:LON, :] = s_ref[v // 3, at : at + LON - to, :]
                t_ref[0 : to + 12 - LON, :] = s_ref[v // 3, at + LON - to : at + 12, :]
        turned = nt(same, t_ref[...].astype(BF16)).astype(BF16)
        out_ref[0, r] = turned[:HEAD]
        out_ref[1, r] = turned[HEAD:]


def join_pieces(pieces, passed, after):
    after = tuple(passed) + tuple(after)
    return pl.pallas_call(
        behind(join_kernel, len(after), 1, len(passed), 2),
        out_shape=(
            jax.ShapeDtypeStruct((2, 12, HEAD, LON), BF16),
            jax.ShapeDtypeStruct((1, 128), F32),
        )
        + tuple(jax.ShapeDtypeStruct(p.shape, p.dtype) for p in passed),
        in_specs=vmem(1) + waits(after),
        out_specs=tuple(vmem(2) + waits(passed)),
        input_output_aliases={1 + i: 2 + i for i in range(len(passed))},
        scratch_shapes=[pltpu.VMEM((16, 6 * HALF, 128), F32), pltpu.VMEM((LON, 128), F32)],
        compiler_params=params(32),
        cost_estimate=cost(2e9, 4e6),
        name="join_pieces",
    )(pieces, *after)


def device_index(x, y, z, core):
    return ((z * 2 + x % 2) * 4 + y) * 4 + (x // 2) * 2 + core


def swapped(z=0, x=0, y=0, core=0):
    pairs = []
    for px in range(4):
        for py in range(4):
            for pz in range(4):
                for c in range(2):
                    to = device_index(px ^ x, py ^ y, pz ^ z, c ^ core)
                    pairs.append((device_index(px, py, pz, c), to))
    return sorted(pairs)


class Sum:
    def __init__(self, keep, got):
        self.tail = (8, keep.shape[-1])
        self.spots = {n: (0, 1, 2, 3) for n in "yzx"}
        self.whole = {n: {e: e for e in range(4)} for n in "yzx"}
        self.terms = [(keep.reshape((4, 4, 4) + self.tail), self.whole, 0)]
        self.terms.append((got.reshape((4, 4, 4) + self.tail), self.whole, 0))

    def columns(self, low, high):
        part = Sum.__new__(Sum)
        part.tail, part.whole, part.spots = (8, high - low), self.whole, dict(self.spots)
        part.terms = [(a, places, low) for a, places, _ in self.terms]
        return part

    def cut(self, name, chosen):
        total = None
        spots = dict(self.spots)
        spots[name] = chosen
        for array, places, low in self.terms:
            index = tuple(
                slice(places[n][spots[n][0]], places[n][spots[n][-1]] + 1) for n in "yzx"
            )
            piece = array[index + (slice(None), slice(low, low + self.tail[1]))]
            total = piece if total is None else total + piece
        return total

    def offer(self, name, by):
        if len(self.spots[name]) == 4:
            give, rest = ((1, 2), (0, 3)) if by == 1 else ((2, 3), (0, 1))
        else:
            give, rest = (by,), (0,)
        piece = self.cut(name, give)
        self.spots[name] = rest
        places = {n: {e: i for i, e in enumerate(self.spots[n])} for n in "yzx"}
        places[name] = {e ^ by: i for i, e in enumerate(give)}
        return piece, places

    def ring_y(self, y, after=()):
        (keep, _, _), (got, _, _) = self.terms
        total = ordered_sum(keep, got, y, after)
        rest = total.reshape(4 * 128, self.tail[1])
        rest = lax.psum_scatter(rest, "lon", scatter_dimension=0, axis_index_groups=Y_RINGS, tiled=True)
        self.reduced = rest
        self.spots["y"] = (0,)
        places = dict(self.whole)
        places["y"] = {0: 0}
        self.terms = [(rest.reshape((1, 4, 4) + self.tail), places, 0)]
        return total

    def cells(self):
        found = []
        for array, places, low in self.terms:
            at = places["y"][0] * array.shape[1] + places["z"][0]
            found.append((array.reshape(-1, 32, array.shape[-1]), at, low // self.tail[1]))
        return found


Y_RINGS = [[c, c + 4, c + 8, c + 12] for c in range(4)]


def exchange(sums, name, by):
    offers = [s.offer(name, by) for s in sums]
    flat = [piece.reshape((-1,) + piece.shape[3:]) for piece, _ in offers]
    out = flat[0] if len(flat) == 1 else jnp.concatenate(flat, axis=-1)
    got = lax.ppermute(out, AXES, swapped(**{name: by}))
    at = 0
    for s, (piece, places) in zip(sums, offers):
        wide = piece.shape[-1]
        s.terms.append((got.reshape(piece.shape[:3] + (8, -1)), places, at))
        at += wide
    return out, got


def add_kernel(y_ref, a_ref, b_ref, *refs):
    out_ref = refs[-1]
    out_ref[...] = a_ref[...] + b_ref[...]


def ordered_sum(a, b, y, after):
    a, b = (t.reshape(4, 128, t.shape[-1]) for t in (a, b))
    block = (1,) + a.shape[1:]
    return pl.pallas_call(
        add_kernel,
        grid_spec=pltpu.PrefetchScalarGridSpec(
            num_scalar_prefetch=1,
            grid=(4,),
            in_specs=[pl.BlockSpec(block, lambda i, y: (i ^ y[0], 0, 0))] * 2 + waits(after),
            out_specs=pl.BlockSpec(block, lambda i, y: (i, 0, 0)),
        ),
        out_shape=jax.ShapeDtypeStruct(a.shape, F32),
        compiler_params=params(16),
        cost_estimate=cost(0, 5e6),
        name="ordered_sum",
    )(y, a, b, *after)


def last_cut_kernel(counts, *refs):
    ins, gain_ref, outs = refs[: sum(counts)], refs[sum(counts)], refs[sum(counts) + 1 :]
    at, col = 0, 0
    for n in counts:
        total = ins[at][0]
        for r in ins[at + 1 : at + n]:
            total = total + r[0]
        wide = total.shape[-1]
        for e in range(4):
            outs[e][:, col : col + wide] = total[8 * e : 8 * e + 8]
        at, col = at + n, col + wide
    row = lax.broadcasted_iota(jnp.int32, (8, 128), 0)
    outs[1][:, col:] = jnp.where(row == 0, gain_ref[...], 0.0)


def last_cut(parts, gain):
    cells = [t.cells() for t in parts]
    counts = tuple(len(c) for c in cells)
    widths = [t.tail[1] for t, c in zip(parts, cells) for _ in c]
    cells = sum(cells, [])
    whole = lambda shape: pl.BlockSpec(shape, lambda i: (0, 0))
    wide = [4 * D, 4 * D + 128, 4 * D, 4 * D]
    return pl.pallas_call(
        functools.partial(last_cut_kernel, counts),
        grid=(1,),
        in_specs=[
            pl.BlockSpec((1, 32, wide), functools.partial(lambda at, col, i: (at, 0, col), at, col))
            for (_, at, col), wide in zip(cells, widths)
        ]
        + [whole((1, 128))],
        out_specs=tuple(whole((8, w)) for w in wide),
        out_shape=tuple(jax.ShapeDtypeStruct((8, w), F32) for w in wide),
        compiler_params=params(24),
        cost_estimate=cost(0, 5e6),
        name="last_cut",
    )(*[a for a, _, _ in cells], gain)


def quarter_kernel(own, got1, got2, got3, gain_ref, z_ref, out_ref, s0, s1, s2, s3, q_ref):
    total = own[...] + got1[:, : 4 * D] + got2[...] + got3[...]
    for g in range(GROUPS):
        for part in range(3):
            at = part * D + g * GW
            out_ref[:, at : at + GW] = total[:, g * D + part * GW : g * D + part * GW + GW]
        q_ref[g] = total[:, g * D + 3 * GW : g * D + D]
    gain = jnp.broadcast_to(gain_ref[...] + got1[0:1, 4 * D :], (8, 128))
    for d, send in enumerate((s0, s1, s2, s3)):
        send[:, :GW] = q_ref[z_ref[0] ^ d]
        send[:, GW:] = gain


def quarters_of(own, got, gain, z):
    return pl.pallas_call(
        quarter_kernel,
        out_shape=(jax.ShapeDtypeStruct((8, 3 * D), F32),)
        + (jax.ShapeDtypeStruct((8, GW + 128), F32),) * 4,
        in_specs=vmem(5) + [pl.BlockSpec(memory_space=pltpu.SMEM)],
        out_specs=tuple(vmem(5)),
        scratch_shapes=[pltpu.VMEM((4, 8, GW), F32)],
        compiler_params=params(16),
        cost_estimate=cost(0, 1e6),
        name="quarters_of",
    )(own, *got, gain, z)


def gather_kernel(m0, m1, m2, m3, z_ref, out_ref, gain_ref, q_ref):
    gain = None
    for d, m in enumerate((m0, m1, m2, m3)):
        q_ref[d] = m[:, :GW]
        term = m[0:1, GW:]
        gain = term if gain is None else gain + term
    for e in range(4):
        out_ref[:, e * GW : e * GW + GW] = q_ref[z_ref[0] ^ e]
    gain_ref[...] = gain


def gather_quarters(pieces, z):
    return pl.pallas_call(
        gather_kernel,
        out_shape=(jax.ShapeDtypeStruct((8, D), F32), jax.ShapeDtypeStruct((1, 128), F32)),
        in_specs=vmem(4) + [pl.BlockSpec(memory_space=pltpu.SMEM)],
        out_specs=tuple(vmem(2)),
        scratch_shapes=[pltpu.VMEM((4, 8, GW), F32)],
        compiler_params=params(16),
        cost_estimate=cost(0, 1e6),
        name="gather_quarters",
    )(*pieces, z)


def row_picks():
    lat, lon = lax.axis_index("lat"), lax.axis_index("lon")
    z, xl = lat // 2, lat % 2
    y, xh, c = lon // 4, (lon // 2) % 2, lon % 2
    x = xh * 2 + xl
    i = jnp.arange(D, dtype=jnp.int32)
    tc = c ^ (i // 512)
    ty = y ^ ((i // 128) % 4)
    tz = z ^ ((i // 32) % 4)
    tx = x ^ ((i // 8) % 4)
    block = ((tz * 2 + tx % 2) * 4 + ty) * 4 + (tx // 2) * 2 + tc
    source = block * 8 + i % 8
    i = jnp.arange(GW, dtype=jnp.int32)
    tc = c ^ (i // 128)
    ty = y ^ ((i // 32) % 4)
    tx = x ^ ((i // 8) % 4)
    block = ((tx % 2) * 4 + ty) * 4 + (tx // 2) * 2 + tc
    group = block * 8 + i % 8
    return tuple(
        (t[:, None] == jnp.arange(t.shape[0], dtype=jnp.int32)[None, :]).astype(BF16)
        for t in (source, group)
    )


def gain_mix():
    i = jnp.arange(D, dtype=jnp.int32)
    source = ((i // 8) % 8) * 128 + (i // 64) * 8 + i % 8
    return (jnp.arange(D, dtype=jnp.int32)[:, None] == source[None, :]).astype(BF16)


def window_order(a):
    a = a.reshape((2, 2, 6, 3, 12) + a.shape[3:])
    return a.transpose((1, 3, 0, 2, 4) + tuple(range(5, a.ndim)))


def per_device(latents, land_mask, norm_gain, qkv_weight, out_weight, out_cotangent):
    lon_index = lax.axis_index("lon")
    pieces = split_pieces(latents.transpose(0, 1, 3, 2))
    pieces = lax.all_to_all(pieces, "lon", split_axis=0, concat_axis=0, tiled=True)
    pick, pick_group = row_picks()
    z_index = (lax.axis_index("lat") // 2).reshape(1)
    mask = jnp.roll(land_mask, -SHIFT, axis=2)
    mask = lax.dynamic_slice_in_dim(mask, lon_index * 36, 36, 2)
    mask = jnp.where(window_order(mask).reshape(TOK, 1) == 1, 0.0, -1e30).astype(F32)
    up = window_order(out_cotangent).reshape(TOK, D)
    gain = norm_gain.reshape(1, D)
    x, scaled, scaled_t = enter(pieces, gain, pick)
    y_index = (lon_index // 4).reshape(1)
    att, grads = [], []

    def heads(g, after):
        a, d, keep, send = attend(
            g, scaled, scaled_t, up, qkv_weight, out_weight, mask, pick_group, z_index, after
        )
        att.append(a)
        grads.append(d)
        return Sum(keep, lax.ppermute(send, AXES, swapped(core=1)))

    def newest(t):
        return t.terms[-1][0]

    s0 = heads(0, ())
    s1 = heads(1, ())
    total = s0.ring_y(y_index)
    s2 = heads(2, (total,))
    total = s1.ring_y(y_index, (att[2],))
    s3 = heads(3, (total, s0.reduced))
    total = s2.ring_y(y_index, (att[3],))
    norm_grad = product(grads, qkv_weight, (total,))
    s3, s4 = s3.columns(0, 2 * GW), s3.columns(2 * GW, 4 * GW)
    out3, _ = exchange([s3], "z", 1)
    out4, _ = exchange([s4], "z", 3)
    leaving = leave(norm_grad, x, up, gain, gain_mix(), (out3, out4, s1.reduced))
    back = lax.all_to_all(leaving, "lon", split_axis=0, concat_axis=0, tiled=True)
    def hand(sums, arrays):
        for t, p in zip(sums, arrays):
            t.terms[-1] = (p,) + t.terms[-1][1:]

    waiting = (s3, s4)
    block, *passed = block_sum(att, x, out_weight, [newest(t) for t in waiting], (leaving,))
    hand(waiting, passed)
    exchange([s3], "z", 3)
    exchange([s4], "z", 1)
    exchange([s3, s4], "y", 1)
    exchange([s0, s1, s2], "z", 1)
    joined, gain_sum, one, two = join_pieces(back, (newest(s3), newest(s0)), (block,))
    hand((s3, s4, s0, s1, s2), (one, one, two, two, two))
    exchange([s3, s4], "y", 3)
    exchange([s0, s1, s2], "z", 3)
    own, *send = last_cut((s0, s1, s2, s3, s4), gain_sum)
    got = [lax.ppermute(a, AXES, swapped(x=d)) for d, a in zip((1, 2, 3), send)]
    qkv_weight_grad, own, *send = quarters_of(own, got, gain_sum, z_index)
    got = [lax.ppermute(a, AXES, swapped(z=d)) for d, a in zip((1, 2, 3), send)]
    out_weight_grad, gain_sum = gather_quarters([own] + got, z_index)
    at = (lon_index % 2) * 64 + lax.axis_index("lat") * 8
    gain_grad = lax.dynamic_slice_in_dim(gain_sum.reshape(128), at, 8, 0)
    block = block.reshape(2, 3, 2, 6, 12, D).transpose(2, 0, 3, 1, 4, 5).reshape(2, 12, 36, D)
    latent_grad = joined.transpose(0, 1, 3, 2)
    return (block, latent_grad, qkv_weight_grad, out_weight_grad, gain_grad)


def solution(mesh):
    return jax.shard_map(
        per_device,
        mesh=mesh,
        in_specs=(
            P(None, "lat", None, "lon"),
            P(None, "lat", None),
            P(),
            P(),
            P(),
            P(None, "lat", "lon", None),
        ),
        out_specs=(
            P(None, "lat", "lon", None),
            P(None, "lat", None, "lon"),
            P(("lat", "lon"), None),
            P(("lat", "lon"), None),
            P(("lat", "lon")),
        ),
        check_vma=False,
    )
```

```python
import functools

import jax
import jax.numpy as jnp
from jax import lax
from jax.experimental import pallas as pl
from jax.experimental.pallas import tpu as pltpu
from jax.sharding import PartitionSpec as P

F32 = jnp.float32
BF16 = jnp.bfloat16
D = 1024
HEAD = 64
WIN = 144
HALF = 72
WINS = 6
TOK = WIN * WINS
SHIFT = 6
LON = 576
GROUPS = 4
ROWS = 6 * HALF + 16
GW = D // GROUPS
QUADS = GW // HEAD
SCALE = HEAD**-0.5
LOG2E = 1.4426950408889634
MIB = 1 << 20
AXES = ("lat", "lon")


def nn(a, b):
    return lax.dot_general(a, b, (((1,), (0,)), ((), ())), preferred_element_type=F32)


def nt(a, b):
    return lax.dot_general(a, b, (((1,), (1,)), ((), ())), preferred_element_type=F32)


def params(mib):
    return pltpu.CompilerParams(vmem_limit_bytes=mib * MIB)


def cost(flops, nbytes):
    return pl.CostEstimate(flops=int(flops / 10), bytes_accessed=int(nbytes / 10), transcendentals=0)


def waits(after):
    return [pl.BlockSpec(memory_space=pl.ANY)] * len(after)


def behind(kernel, count, operands, passed=0, results=1):
    def body(*refs):
        rest = refs[operands + count :]
        kernel(*refs[:operands], *rest[:results], *rest[results + passed :])

    return body


def vmem(n):
    return [pl.BlockSpec(memory_space=pltpu.VMEM)] * n


def split_kernel(z_ref, out_ref, t_ref, s_ref):
    row = lax.broadcasted_iota(jnp.int32, (LON, LON), 0)
    col = lax.broadcasted_iota(jnp.int32, (LON, LON), 1)
    source = row + SHIFT
    source = jnp.where(source >= LON, source - LON, source)
    pick = (col == source).astype(BF16)
    for r in range(12):
        both = jnp.concatenate([z_ref[0, r], z_ref[1, r]], axis=0)
        t_ref[...] = nt(pick, both)
        for v in range(48):
            at = ((r // 6) * 3 + v % 3) * HALF + (r % 6) * 12
            s_ref[v // 3, at : at + 12, :] = t_ref[12 * v : 12 * v + 12, :]
    for k in range(16):
        out_ref[k] = s_ref[k].astype(BF16)


def split_pieces(z):
    return pl.pallas_call(
        split_kernel,
        out_shape=jax.ShapeDtypeStruct((16, 6 * HALF, 128), BF16),
        in_specs=vmem(1),
        out_specs=vmem(1)[0],
        scratch_shapes=[pltpu.VMEM((LON, 128), F32), pltpu.VMEM((16, 6 * HALF, 128), F32)],
        compiler_params=params(32),
        cost_estimate=cost(2e9, 4e6),
        name="split_pieces",
    )(z)


def norm_parts(x):
    centred = x - jnp.sum(x, axis=-1, keepdims=True) * (1.0 / D)
    variance = jnp.sum(centred * centred, axis=-1, keepdims=True) * (1.0 / D)
    inv_scale = lax.rsqrt(variance + 1e-05)
    return centred * inv_scale, inv_scale


def enter_kernel(r_ref, gain_ref, pick_ref, x_ref, scaled_ref, scaled_t_ref, xs_ref):
    low = lax.broadcasted_iota(jnp.int32, (6 * HALF, 128), 1) < HEAD
    for p in range(8):
        first = r_ref[2 * p].astype(F32)
        second = r_ref[2 * p + 1].astype(F32)
        level0 = jnp.where(low, first, pltpu.roll(second, HEAD, 1))
        level1 = jnp.where(low, pltpu.roll(first, HEAD, 1), second)
        for w in range(WINS):
            at = w * WIN
            xs_ref[at : at + HALF, 128 * p : 128 * p + 128] = level0[HALF * w : HALF * w + HALF]
            xs_ref[at + HALF : at + WIN, 128 * p : 128 * p + 128] = level1[HALF * w : HALF * w + HALF]

    def rows(i, _):
        at = pl.ds(pl.multiple_of(i * 48, 48), 48)
        x = xs_ref[at, :]
        x_ref[at, :] = x.astype(BF16)
        normed, _ = norm_parts(x)
        scaled_ref[at, :] = (normed * gain_ref[...]).astype(BF16)
        return 0

    lax.fori_loop(0, TOK // 48, rows, 0)

    def turn(i, _):
        at = pl.ds(pl.multiple_of(i * 256, 256), 256)
        scaled_t_ref[at, :] = nt(pick_ref[at, :], scaled_ref[...]).astype(BF16)
        return 0

    lax.fori_loop(0, 4, turn, 0)


def enter(pieces, gain, pick):
    return pl.pallas_call(
        enter_kernel,
        out_shape=(
            jax.ShapeDtypeStruct((TOK, D), BF16),
            jax.ShapeDtypeStruct((TOK, D), BF16),
            jax.ShapeDtypeStruct((D, TOK), BF16),
        ),
        in_specs=vmem(3),
        out_specs=tuple(vmem(3)),
        scratch_shapes=[pltpu.VMEM((TOK, D), F32)],
        compiler_params=params(32),
        cost_estimate=cost(3e9, 9e6),
        name="enter",
    )(pieces, gain, pick)


def attend_kernel(
    scaled_ref, scaled_t_ref, up_ref, wq_ref, wk_ref, wv_ref, wo_ref, mask_ref,
    pick_ref, z_ref, att_ref, grad_ref, keep_ref, send_ref, q_ref, k_ref, v_ref, o_ref, other_ref,
):
    for w_ref, p_ref in ((wq_ref, q_ref), (wk_ref, k_ref), (wv_ref, v_ref)):
        p_ref[...] = nn(scaled_ref[...], w_ref[...]).astype(BF16)
    o_ref[...] = nt(up_ref[...], wo_ref[...]).astype(BF16)

    wide = (WIN, QUADS * WIN)
    key = lax.broadcasted_iota(jnp.int32, wide, 0)
    query = lax.broadcasted_iota(jnp.int32, wide, 1)
    same = query == key
    for h in range(1, QUADS):
        same = same | (query == key + h * WIN)
    other_ref[...] = jnp.where(same, 0.0, 1.0)
    lane = lax.broadcasted_iota(jnp.int32, (WIN, GW), 1)
    mine = [(lane >= HEAD * h) & (lane < HEAD * h + HEAD) for h in range(QUADS)]
    zero = jnp.zeros((WIN, GW), BF16)

    def by_head(a):
        return jnp.concatenate([jnp.where(m, a, zero) for m in mine], axis=0)

    def own_head(a):
        total = a[:WIN]
        for h in range(1, QUADS):
            total = jnp.where(mine[h], a[h * WIN : h * WIN + WIN], total)
        return total

    def window(i, _):
        at = pl.ds(pl.multiple_of(i * WIN, WIN), WIN)
        k, v = k_ref[at, :], v_ref[at, :]
        q, o = by_head(q_ref[at, :]), by_head(o_ref[at, :])
        scores = nt(k, q) * (SCALE * LOG2E) + other_ref[...] * mask_ref[at, :]
        raised = jnp.exp2(scores - jnp.max(scores, axis=0, keepdims=True))
        prob = raised * (1.0 / jnp.sum(raised, axis=0, keepdims=True))
        prob_half = prob.astype(BF16)
        prob_grad = nt(v, o)
        inner = jnp.sum(prob * prob_grad, axis=0, keepdims=True)
        score_grad = (prob * (prob_grad - inner)).astype(BF16)
        att_ref[at, :] = own_head(nn(prob_half.T, v)).astype(BF16)
        grad_ref[at, 0:GW] = (own_head(nn(score_grad.T, k)) * SCALE).astype(BF16)
        grad_ref[at, GW : 2 * GW] = (nn(score_grad, q) * SCALE).astype(BF16)
        grad_ref[at, 2 * GW : 3 * GW] = nn(prob_half, o).astype(BF16)
        return 0

    lax.fori_loop(0, WINS, window, 0)

    def weights(i, _):
        at = pl.ds(pl.multiple_of(i * 256, 256), 256)
        keep_ref[at, 0 : 3 * GW] = nn(scaled_t_ref[at, :], grad_ref[...])
        far = pl.ds(pl.multiple_of(i * 256 + 512, 256), 256)
        send_ref[at, 0 : 3 * GW] = nn(scaled_t_ref[far, :], grad_ref[...])
        return 0

    lax.fori_loop(0, 2, weights, 0)

    turned = nt(pick_ref[...], att_ref[...]).astype(BF16)
    for e in range(4):
        cols = pl.ds(pl.multiple_of((z_ref[0] ^ e) * GW, GW), GW)
        part = nn(turned, up_ref[:, cols])
        for y in range(4):
            at = 128 * y + 32 * e
            keep_ref[at : at + 32, 3 * GW :] = part[32 * y : 32 * y + 32]
            send_ref[at : at + 32, 3 * GW :] = part[128 + 32 * y : 160 + 32 * y]


def attend(g, scaled, scaled_t, up, qkv_weight, out_weight, mask, pick, z, after=()):
    full = lambda shape: pl.BlockSpec(shape, lambda i: (0, 0))
    return pl.pallas_call(
        behind(attend_kernel, len(after), 10),
        grid=(1,),
        out_shape=(
            jax.ShapeDtypeStruct((TOK, GW), BF16),
            jax.ShapeDtypeStruct((TOK, 3 * GW), BF16),
            jax.ShapeDtypeStruct((D // 2, 4 * GW), F32),
            jax.ShapeDtypeStruct((D // 2, 4 * GW), F32),
        ),
        in_specs=[
            full((TOK, D)),
            full((D, TOK)),
            full((TOK, D)),
            pl.BlockSpec((D, GW), lambda i: (0, g)),
            pl.BlockSpec((D, GW), lambda i: (0, GROUPS + g)),
            pl.BlockSpec((D, GW), lambda i: (0, 2 * GROUPS + g)),
            pl.BlockSpec((GW, D), lambda i: (g, 0)),
            full((TOK, 1)),
            full((GW, GW)),
            pl.BlockSpec(memory_space=pltpu.SMEM),
        ]
        + waits(after),
        out_specs=(
            full((TOK, GW)),
            full((TOK, 3 * GW)),
            full((D // 2, 4 * GW)),
            full((D // 2, 4 * GW)),
        ),
        scratch_shapes=[pltpu.VMEM((TOK, GW), BF16)] * 4 + [pltpu.VMEM((WIN, QUADS * WIN), F32)],
        compiler_params=params(48),
        cost_estimate=cost(8e9, 15e6),
        name="attend",
    )(scaled, scaled_t, up, qkv_weight, qkv_weight, qkv_weight, out_weight, mask, pick, z, *after)


def gate_kernel(out_ref):
    out_ref[...] = jnp.zeros((8, 128), F32)


def gate(passed, after):
    return pl.pallas_call(
        behind(gate_kernel, len(passed) + len(after), 0, len(passed)),
        out_shape=(jax.ShapeDtypeStruct((8, 128), F32),)
        + tuple(jax.ShapeDtypeStruct(p.shape, p.dtype) for p in passed),
        in_specs=waits(passed) + waits(after),
        out_specs=tuple(vmem(1) + waits(passed)),
        input_output_aliases={i: 1 + i for i in range(len(passed))},
        compiler_params=params(4),
        cost_estimate=cost(0, 1e4),
        name="gate",
    )(*passed, *after)[1:]


def block_kernel(a0, a1, a2, a3, x_ref, w_ref, out_ref):
    def rows(i, _):
        at = pl.ds(pl.multiple_of(i * 432, 432), 432)
        total = x_ref[at, :].astype(F32)
        for g, a in enumerate((a0, a1, a2, a3)):
            total = total + nn(a[at, :], w_ref[GW * g : GW * g + GW, :])
        out_ref[at, :] = total.astype(BF16)
        return 0

    lax.fori_loop(0, 2, rows, 0)


def block_sum(att, x, out_weight, after):
    return pl.pallas_call(
        behind(block_kernel, len(after), 6),
        out_shape=jax.ShapeDtypeStruct((TOK, D), BF16),
        in_specs=vmem(6) + waits(after),
        out_specs=vmem(1)[0],
        compiler_params=params(32),
        cost_estimate=cost(2e9, 8e6),
        name="block_sum",
    )(*att, x, out_weight, *after)


def product_kernel(g0, g1, g2, g3, w_ref, n_ref):
    def product(i, _):
        at = pl.ds(pl.multiple_of(i * 432, 432), 432)
        total = None
        for g, d in enumerate((g0, g1, g2, g3)):
            for part in range(3):
                base = part * D + g * GW
                piece = nt(d[at, part * GW : part * GW + GW], w_ref[:, base : base + GW])
                total = piece if total is None else total + piece
        n_ref[at, :] = total
        return 0

    lax.fori_loop(0, 2, product, 0)


def product(grads, qkv_weight, after=()):
    return pl.pallas_call(
        behind(product_kernel, len(after), 5),
        out_shape=jax.ShapeDtypeStruct((TOK, D), F32),
        in_specs=vmem(5) + waits(after),
        out_specs=vmem(1)[0],
        compiler_params=params(40),
        cost_estimate=cost(6e9, 15e6),
        name="product",
    )(*grads, qkv_weight, *after)


def leave_kernel(s_ref, x_ref, up_ref, gain_ref, mix_ref, out_ref, n_ref, sum_ref):
    step = pl.program_id(0)

    @pl.when(step == 0)
    def _():
        sum_ref[...] = jnp.zeros((8, D), F32)

    def rows(i, gain_sum):
        at = pl.ds(pl.multiple_of(i * 48, 48), 48)
        normed, inv_scale = norm_parts(x_ref[at, :].astype(F32))
        n = s_ref[at, :]
        both = n * normed
        gain = gain_ref[...]
        g = n * gain
        mean_g = jnp.sum(g, axis=-1, keepdims=True) * (1.0 / D)
        mean_gn = jnp.sum(both * gain, axis=-1, keepdims=True) * (1.0 / D)
        n_ref[at, :] = up_ref[at, :].astype(F32) + inv_scale * (g - mean_g - normed * mean_gn)
        return gain_sum + jnp.sum(both.reshape(6, 8, D), axis=0)

    gain_sum = lax.fori_loop(0, 6, rows, sum_ref[...])
    sum_ref[...] = gain_sum

    low = lax.broadcasted_iota(jnp.int32, (WIN, 128), 1) < HEAD
    to = pl.ds(pl.multiple_of(step * WIN, WIN), WIN)
    for p in range(8):
        cols = slice(128 * p, 128 * p + 128)
        level0 = jnp.concatenate([n_ref[0:HALF, cols], n_ref[WIN : WIN + HALF, cols]], axis=0)
        level1 = jnp.concatenate([n_ref[HALF:WIN, cols], n_ref[WIN + HALF : 2 * WIN, cols]], axis=0)
        out_ref[2 * p, to] = jnp.where(low, level0, pltpu.roll(level1, HEAD, 1)).astype(BF16)
        out_ref[2 * p + 1, to] = jnp.where(low, pltpu.roll(level0, HEAD, 1), level1).astype(BF16)

    @pl.when(step == 2)
    def _():
        whole = jnp.sum(gain_sum, axis=0, keepdims=True)
        high = whole.astype(BF16).astype(F32)
        mid = (whole - high).astype(BF16).astype(F32)
        row16 = lax.broadcasted_iota(jnp.int32, (16, D), 0)
        split = jnp.where(row16 == 0, high, jnp.where(row16 == 1, mid, whole - high - mid))
        split = jnp.where(row16 < 3, split, 0.0).astype(BF16)
        split = nn(split, mix_ref[...]).astype(BF16)
        for k in range(16):
            out_ref[k, 6 * HALF :] = split[:, 128 * (k // 2) : 128 * (k // 2) + 128]


def leave(norm_grad, x, up, gain, mix, after=()):
    full = lambda shape: pl.BlockSpec(shape, lambda i: (0,) * len(shape))
    part = pl.BlockSpec((2 * WIN, D), lambda i: (i, 0))
    return pl.pallas_call(
        behind(leave_kernel, len(after), 5),
        grid=(3,),
        out_shape=jax.ShapeDtypeStruct((16, ROWS, 128), BF16),
        in_specs=[part, part, part, full((1, D)), full((D, D))] + waits(after),
        out_specs=full((16, ROWS, 128)),
        scratch_shapes=[pltpu.VMEM((2 * WIN, D), F32), pltpu.VMEM((8, D), F32)],
        compiler_params=params(32),
        cost_estimate=cost(4e9, 10e6),
        name="leave",
    )(norm_grad, x, up, gain, mix, *after)


def join_kernel(r_ref, out_ref, gain_ref, s_ref, t_ref):
    gain = None
    for k in range(16):
        s_ref[k] = r_ref[k, 0 : 6 * HALF].astype(F32)
        term = r_ref[k, 6 * HALF :].astype(F32)
        gain = term if gain is None else gain + term
    gain_ref[...] = jnp.sum(gain, axis=0, keepdims=True)
    same = lax.broadcasted_iota(jnp.int32, (128, 128), 0) == lax.broadcasted_iota(
        jnp.int32, (128, 128), 1
    )
    same = same.astype(BF16)
    for r in range(12):
        for v in range(48):
            at = ((r // 6) * 3 + v % 3) * HALF + (r % 6) * 12
            to = 12 * v + SHIFT
            if to + 12 <= LON:
                t_ref[to : to + 12, :] = s_ref[v // 3, at : at + 12, :]
            else:
                t_ref[to:LON, :] = s_ref[v // 3, at : at + LON - to, :]
                t_ref[0 : to + 12 - LON, :] = s_ref[v // 3, at + LON - to : at + 12, :]
        turned = nt(same, t_ref[...].astype(BF16)).astype(BF16)
        out_ref[0, r] = turned[:HEAD]
        out_ref[1, r] = turned[HEAD:]


def join_pieces(pieces, passed, after):
    after = tuple(passed) + tuple(after)
    return pl.pallas_call(
        behind(join_kernel, len(after), 1, len(passed), 2),
        out_shape=(
            jax.ShapeDtypeStruct((2, 12, HEAD, LON), BF16),
            jax.ShapeDtypeStruct((1, 128), F32),
        )
        + tuple(jax.ShapeDtypeStruct(p.shape, p.dtype) for p in passed),
        in_specs=vmem(1) + waits(after),
        out_specs=tuple(vmem(2) + waits(passed)),
        input_output_aliases={1 + i: 2 + i for i in range(len(passed))},
        scratch_shapes=[pltpu.VMEM((16, 6 * HALF, 128), F32), pltpu.VMEM((LON, 128), F32)],
        compiler_params=params(32),
        cost_estimate=cost(2e9, 4e6),
        name="join_pieces",
    )(pieces, *after)


def device_index(x, y, z, core):
    return ((z * 2 + x % 2) * 4 + y) * 4 + (x // 2) * 2 + core


def swapped(z=0, x=0, y=0, core=0):
    pairs = []
    for px in range(4):
        for py in range(4):
            for pz in range(4):
                for c in range(2):
                    to = device_index(px ^ x, py ^ y, pz ^ z, c ^ core)
                    pairs.append((device_index(px, py, pz, c), to))
    return sorted(pairs)


class Sum:
    def __init__(self, keep, got):
        self.tail = (8, keep.shape[-1])
        self.spots = {n: (0, 1, 2, 3) for n in "yzx"}
        self.whole = {n: {e: e for e in range(4)} for n in "yzx"}
        self.terms = [(keep.reshape((4, 4, 4) + self.tail), self.whole, 0)]
        self.terms.append((got.reshape((4, 4, 4) + self.tail), self.whole, 0))

    def columns(self, low, high):
        part = Sum.__new__(Sum)
        part.tail, part.whole, part.spots = (8, high - low), self.whole, dict(self.spots)
        part.terms = [(a, places, low) for a, places, _ in self.terms]
        return part

    def cut(self, name, chosen):
        total = None
        spots = dict(self.spots)
        spots[name] = chosen
        for array, places, low in self.terms:
            index = tuple(
                slice(places[n][spots[n][0]], places[n][spots[n][-1]] + 1) for n in "yzx"
            )
            piece = array[index + (slice(None), slice(low, low + self.tail[1]))]
            total = piece if total is None else total + piece
        return total

    def offer(self, name, by):
        if len(self.spots[name]) == 4:
            give, rest = ((1, 2), (0, 3)) if by == 1 else ((2, 3), (0, 1))
        else:
            give, rest = (by,), (0,)
        piece = self.cut(name, give)
        self.spots[name] = rest
        places = {n: {e: i for i, e in enumerate(self.spots[n])} for n in "yzx"}
        places[name] = {e ^ by: i for i, e in enumerate(give)}
        return piece, places

    def ring_y(self, y, after=()):
        (keep, _, _), (got, _, _) = self.terms
        total = ordered_sum(keep, got, y, after)
        rest = total.reshape(4 * 128, self.tail[1])
        rest = lax.psum_scatter(rest, "lon", scatter_dimension=0, axis_index_groups=Y_RINGS, tiled=True)
        self.reduced = rest
        self.spots["y"] = (0,)
        places = dict(self.whole)
        places["y"] = {0: 0}
        self.terms = [(rest.reshape((1, 4, 4) + self.tail), places, 0)]
        return total

    def cells(self):
        found = []
        for array, places, low in self.terms:
            at = places["y"][0] * array.shape[1] + places["z"][0]
            found.append((array.reshape(-1, 32, array.shape[-1]), at, low // self.tail[1]))
        return found


Y_RINGS = [[c, c + 4, c + 8, c + 12] for c in range(4)]


def exchange(sums, name, by):
    offers = [s.offer(name, by) for s in sums]
    flat = [piece.reshape((-1,) + piece.shape[3:]) for piece, _ in offers]
    out = flat[0] if len(flat) == 1 else jnp.concatenate(flat, axis=-1)
    got = lax.ppermute(out, AXES, swapped(**{name: by}))
    at = 0
    for s, (piece, places) in zip(sums, offers):
        wide = piece.shape[-1]
        s.terms.append((got.reshape(piece.shape[:3] + (8, -1)), places, at))
        at += wide
    return out, got


def add_kernel(y_ref, a_ref, b_ref, *refs):
    out_ref = refs[-1]
    out_ref[...] = a_ref[...] + b_ref[...]


def ordered_sum(a, b, y, after):
    a, b = (t.reshape(4, 128, t.shape[-1]) for t in (a, b))
    block = (1,) + a.shape[1:]
    return pl.pallas_call(
        add_kernel,
        grid_spec=pltpu.PrefetchScalarGridSpec(
            num_scalar_prefetch=1,
            grid=(4,),
            in_specs=[pl.BlockSpec(block, lambda i, y: (i ^ y[0], 0, 0))] * 2 + waits(after),
            out_specs=pl.BlockSpec(block, lambda i, y: (i, 0, 0)),
        ),
        out_shape=jax.ShapeDtypeStruct(a.shape, F32),
        compiler_params=params(16),
        cost_estimate=cost(0, 5e6),
        name="ordered_sum",
    )(y, a, b, *after)


def last_cut_kernel(counts, *refs):
    ins, gain_ref, outs = refs[: sum(counts)], refs[sum(counts)], refs[sum(counts) + 1 :]
    at, col = 0, 0
    for n in counts:
        total = ins[at][0]
        for r in ins[at + 1 : at + n]:
            total = total + r[0]
        wide = total.shape[-1]
        for e in range(4):
            outs[e][:, col : col + wide] = total[8 * e : 8 * e + 8]
        at, col = at + n, col + wide
    row = lax.broadcasted_iota(jnp.int32, (8, 128), 0)
    outs[1][:, col:] = jnp.where(row == 0, gain_ref[...], 0.0)


def last_cut(parts, gain):
    cells = [t.cells() for t in parts]
    counts = tuple(len(c) for c in cells)
    widths = [t.tail[1] for t, c in zip(parts, cells) for _ in c]
    cells = sum(cells, [])
    whole = lambda shape: pl.BlockSpec(shape, lambda i: (0, 0))
    wide = [4 * D, 4 * D + 128, 4 * D, 4 * D]
    return pl.pallas_call(
        functools.partial(last_cut_kernel, counts),
        grid=(1,),
        in_specs=[
            pl.BlockSpec((1, 32, wide), functools.partial(lambda at, col, i: (at, 0, col), at, col))
            for (_, at, col), wide in zip(cells, widths)
        ]
        + [whole((1, 128))],
        out_specs=tuple(whole((8, w)) for w in wide),
        out_shape=tuple(jax.ShapeDtypeStruct((8, w), F32) for w in wide),
        compiler_params=params(24),
        cost_estimate=cost(0, 5e6),
        name="last_cut",
    )(*[a for a, _, _ in cells], gain)


def quarter_kernel(own, got1, got2, got3, gain_ref, z_ref, out_ref, s0, s1, s2, s3, q_ref):
    total = own[...] + got1[:, : 4 * D] + got2[...] + got3[...]
    for g in range(GROUPS):
        for part in range(3):
            at = part * D + g * GW
            out_ref[:, at : at + GW] = total[:, g * D + part * GW : g * D + part * GW + GW]
        q_ref[g] = total[:, g * D + 3 * GW : g * D + D]
    gain = jnp.broadcast_to(gain_ref[...] + got1[0:1, 4 * D :], (8, 128))
    for d, send in enumerate((s0, s1, s2, s3)):
        send[:, :GW] = q_ref[z_ref[0] ^ d]
        send[:, GW:] = gain


def quarters_of(own, got, gain, z):
    return pl.pallas_call(
        quarter_kernel,
        out_shape=(jax.ShapeDtypeStruct((8, 3 * D), F32),)
        + (jax.ShapeDtypeStruct((8, GW + 128), F32),) * 4,
        in_specs=vmem(5) + [pl.BlockSpec(memory_space=pltpu.SMEM)],
        out_specs=tuple(vmem(5)),
        scratch_shapes=[pltpu.VMEM((4, 8, GW), F32)],
        compiler_params=params(16),
        cost_estimate=cost(0, 1e6),
        name="quarters_of",
    )(own, *got, gain, z)


def gather_kernel(m0, m1, m2, m3, z_ref, out_ref, gain_ref, q_ref):
    gain = None
    for d, m in enumerate((m0, m1, m2, m3)):
        q_ref[d] = m[:, :GW]
        term = m[0:1, GW:]
        gain = term if gain is None else gain + term
    for e in range(4):
        out_ref[:, e * GW : e * GW + GW] = q_ref[z_ref[0] ^ e]
    gain_ref[...] = gain


def gather_quarters(pieces, z):
    return pl.pallas_call(
        gather_kernel,
        out_shape=(jax.ShapeDtypeStruct((8, D), F32), jax.ShapeDtypeStruct((1, 128), F32)),
        in_specs=vmem(4) + [pl.BlockSpec(memory_space=pltpu.SMEM)],
        out_specs=tuple(vmem(2)),
        scratch_shapes=[pltpu.VMEM((4, 8, GW), F32)],
        compiler_params=params(16),
        cost_estimate=cost(0, 1e6),
        name="gather_quarters",
    )(*pieces, z)


def row_picks():
    lat, lon = lax.axis_index("lat"), lax.axis_index("lon")
    z, xl = lat // 2, lat % 2
    y, xh, c = lon // 4, (lon // 2) % 2, lon % 2
    x = xh * 2 + xl
    i = jnp.arange(D, dtype=jnp.int32)
    tc = c ^ (i // 512)
    ty = y ^ ((i // 128) % 4)
    tz = z ^ ((i // 32) % 4)
    tx = x ^ ((i // 8) % 4)
    block = ((tz * 2 + tx % 2) * 4 + ty) * 4 + (tx // 2) * 2 + tc
    source = block * 8 + i % 8
    i = jnp.arange(GW, dtype=jnp.int32)
    tc = c ^ (i // 128)
    ty = y ^ ((i // 32) % 4)
    tx = x ^ ((i // 8) % 4)
    block = ((tx % 2) * 4 + ty) * 4 + (tx // 2) * 2 + tc
    group = block * 8 + i % 8
    return tuple(
        (t[:, None] == jnp.arange(t.shape[0], dtype=jnp.int32)[None, :]).astype(BF16)
        for t in (source, group)
    )


def gain_mix():
    i = jnp.arange(D, dtype=jnp.int32)
    source = ((i // 8) % 8) * 128 + (i // 64) * 8 + i % 8
    return (jnp.arange(D, dtype=jnp.int32)[:, None] == source[None, :]).astype(BF16)


def window_order(a):
    a = a.reshape((2, 2, 6, 3, 12) + a.shape[3:])
    return a.transpose((1, 3, 0, 2, 4) + tuple(range(5, a.ndim)))


def per_device(latents, land_mask, norm_gain, qkv_weight, out_weight, out_cotangent):
    lon_index = lax.axis_index("lon")
    pieces = split_pieces(latents.transpose(0, 1, 3, 2))
    pieces = lax.all_to_all(pieces, "lon", split_axis=0, concat_axis=0, tiled=True)
    pick, pick_group = row_picks()
    z_index = (lax.axis_index("lat") // 2).reshape(1)
    mask = jnp.roll(land_mask, -SHIFT, axis=2)
    mask = lax.dynamic_slice_in_dim(mask, lon_index * 36, 36, 2)
    mask = jnp.where(window_order(mask).reshape(TOK, 1) == 1, 0.0, -1e30).astype(F32)
    up = window_order(out_cotangent).reshape(TOK, D)
    gain = norm_gain.reshape(1, D)
    x, scaled, scaled_t = enter(pieces, gain, pick)
    y_index = (lon_index // 4).reshape(1)
    att, grads = [], []

    def heads(g, after):
        a, d, keep, send = attend(
            g, scaled, scaled_t, up, qkv_weight, out_weight, mask, pick_group, z_index, after
        )
        att.append(a)
        grads.append(d)
        return Sum(keep, lax.ppermute(send, AXES, swapped(core=1)))

    def newest(t):
        return t.terms[-1][0]

    s0 = heads(0, ())
    s1 = heads(1, ())
    total = s0.ring_y(y_index)
    s2 = heads(2, (total,))
    total = s1.ring_y(y_index, (att[2],))
    s3 = heads(3, (total, s0.reduced))
    total = s2.ring_y(y_index, (att[3],))
    norm_grad = product(grads, qkv_weight)
    s3, s4 = s3.columns(0, 2 * GW), s3.columns(2 * GW, 4 * GW)
    out3, _ = exchange([s3], "z", 1)
    out4, _ = exchange([s4], "z", 3)
    leaving = leave(norm_grad, x, up, gain, gain_mix(), (out3, out4, s1.reduced, total))
    back = lax.all_to_all(leaving, "lon", split_axis=0, concat_axis=0, tiled=True)
    def hand(sums, arrays):
        for t, p in zip(sums, arrays):
            t.terms[-1] = (p,) + t.terms[-1][1:]

    waiting = (s3, s4)
    passed = gate([newest(t) for t in waiting], (leaving,))
    block = block_sum(att, x, out_weight, (leaving,))
    hand(waiting, passed)
    exchange([s3], "z", 3)
    exchange([s4], "z", 1)
    exchange([s3, s4], "y", 1)
    exchange([s0, s1, s2], "z", 1)
    joined, gain_sum, one = join_pieces(back, (newest(s3),), (block,))
    hand((s3, s4), (one, one))
    exchange([s3, s4], "y", 3)
    exchange([s0, s1, s2], "z", 3)
    own, *send = last_cut((s0, s1, s2, s3, s4), gain_sum)
    got = [lax.ppermute(a, AXES, swapped(x=d)) for d, a in zip((1, 2, 3), send)]
    qkv_weight_grad, own, *send = quarters_of(own, got, gain_sum, z_index)
    got = [lax.ppermute(a, AXES, swapped(z=d)) for d, a in zip((1, 2, 3), send)]
    out_weight_grad, gain_sum = gather_quarters([own] + got, z_index)
    at = (lon_index % 2) * 64 + lax.axis_index("lat") * 8
    gain_grad = lax.dynamic_slice_in_dim(gain_sum.reshape(128), at, 8, 0)
    block = block.reshape(2, 3, 2, 6, 12, D).transpose(2, 0, 3, 1, 4, 5).reshape(2, 12, 36, D)
    latent_grad = joined.transpose(0, 1, 3, 2)
    return (block, latent_grad, qkv_weight_grad, out_weight_grad, gain_grad)


def solution(mesh):
    return jax.shard_map(
        per_device,
        mesh=mesh,
        in_specs=(
            P(None, "lat", None, "lon"),
            P(None, "lat", None),
            P(),
            P(),
            P(),
            P(None, "lat", "lon", None),
        ),
        out_specs=(
            P(None, "lat", "lon", None),
            P(None, "lat", None, "lon"),
            P(("lat", "lon"), None),
            P(("lat", "lon"), None),
            P(("lat", "lon")),
        ),
        check_vma=False,
    )
```

```python
import functools

import jax
import jax.numpy as jnp
from jax import lax
from jax.experimental import pallas as pl
from jax.experimental.pallas import tpu as pltpu
from jax.sharding import PartitionSpec as P

F32 = jnp.float32
BF16 = jnp.bfloat16
D = 1024
HEAD = 64
WIN = 144
HALF = 72
WINS = 6
TOK = WIN * WINS
SHIFT = 6
LON = 576
GROUPS = 4
ROWS = 6 * HALF + 16
GW = D // GROUPS
QUADS = GW // HEAD
SCALE = HEAD**-0.5
LOG2E = 1.4426950408889634
MIB = 1 << 20
AXES = ("lat", "lon")


def nn(a, b):
    return lax.dot_general(a, b, (((1,), (0,)), ((), ())), preferred_element_type=F32)


def nt(a, b):
    return lax.dot_general(a, b, (((1,), (1,)), ((), ())), preferred_element_type=F32)


def params(mib):
    return pltpu.CompilerParams(vmem_limit_bytes=mib * MIB)


def cost(flops, nbytes):
    return pl.CostEstimate(flops=int(flops / 10), bytes_accessed=int(nbytes / 10), transcendentals=0)


def waits(after):
    return [pl.BlockSpec(memory_space=pl.ANY)] * len(after)


def behind(kernel, count, operands, passed=0, results=1):
    def body(*refs):
        rest = refs[operands + count :]
        kernel(*refs[:operands], *rest[:results], *rest[results + passed :])

    return body


def vmem(n):
    return [pl.BlockSpec(memory_space=pltpu.VMEM)] * n


def split_kernel(z_ref, out_ref, t_ref, s_ref):
    row = lax.broadcasted_iota(jnp.int32, (LON, LON), 0)
    col = lax.broadcasted_iota(jnp.int32, (LON, LON), 1)
    source = row + SHIFT
    source = jnp.where(source >= LON, source - LON, source)
    pick = (col == source).astype(BF16)
    for r in range(12):
        both = jnp.concatenate([z_ref[0, r], z_ref[1, r]], axis=0)
        t_ref[...] = nt(pick, both)
        for v in range(48):
            at = ((r // 6) * 3 + v % 3) * HALF + (r % 6) * 12
            s_ref[v // 3, at : at + 12, :] = t_ref[12 * v : 12 * v + 12, :]
    for k in range(16):
        out_ref[k] = s_ref[k].astype(BF16)


def split_pieces(z):
    return pl.pallas_call(
        split_kernel,
        out_shape=jax.ShapeDtypeStruct((16, 6 * HALF, 128), BF16),
        in_specs=vmem(1),
        out_specs=vmem(1)[0],
        scratch_shapes=[pltpu.VMEM((LON, 128), F32), pltpu.VMEM((16, 6 * HALF, 128), F32)],
        compiler_params=params(32),
        cost_estimate=cost(2e9, 4e6),
        name="split_pieces",
    )(z)


def norm_parts(x):
    centred = x - jnp.sum(x, axis=-1, keepdims=True) * (1.0 / D)
    variance = jnp.sum(centred * centred, axis=-1, keepdims=True) * (1.0 / D)
    inv_scale = lax.rsqrt(variance + 1e-05)
    return centred * inv_scale, inv_scale


def enter_kernel(r_ref, gain_ref, pick_ref, x_ref, scaled_ref, scaled_t_ref, xs_ref):
    low = lax.broadcasted_iota(jnp.int32, (6 * HALF, 128), 1) < HEAD
    for p in range(8):
        first = r_ref[2 * p].astype(F32)
        second = r_ref[2 * p + 1].astype(F32)
        level0 = jnp.where(low, first, pltpu.roll(second, HEAD, 1))
        level1 = jnp.where(low, pltpu.roll(first, HEAD, 1), second)
        for w in range(WINS):
            at = w * WIN
            xs_ref[at : at + HALF, 128 * p : 128 * p + 128] = level0[HALF * w : HALF * w + HALF]
            xs_ref[at + HALF : at + WIN, 128 * p : 128 * p + 128] = level1[HALF * w : HALF * w + HALF]

    def rows(i, _):
        at = pl.ds(pl.multiple_of(i * 48, 48), 48)
        x = xs_ref[at, :]
        x_ref[at, :] = x.astype(BF16)
        normed, _ = norm_parts(x)
        scaled_ref[at, :] = (normed * gain_ref[...]).astype(BF16)
        return 0

    lax.fori_loop(0, TOK // 48, rows, 0)

    def turn(i, _):
        at = pl.ds(pl.multiple_of(i * 256, 256), 256)
        scaled_t_ref[at, :] = nt(pick_ref[at, :], scaled_ref[...]).astype(BF16)
        return 0

    lax.fori_loop(0, 4, turn, 0)


def enter(pieces, gain, pick):
    return pl.pallas_call(
        enter_kernel,
        out_shape=(
            jax.ShapeDtypeStruct((TOK, D), BF16),
            jax.ShapeDtypeStruct((TOK, D), BF16),
            jax.ShapeDtypeStruct((D, TOK), BF16),
        ),
        in_specs=vmem(3),
        out_specs=tuple(vmem(3)),
        scratch_shapes=[pltpu.VMEM((TOK, D), F32)],
        compiler_params=params(62),
        cost_estimate=cost(3e9, 9e6),
        name="enter",
    )(pieces, gain, pick)


def attend_kernel(
    scaled_ref, scaled_t_ref, up_ref, wq_ref, wk_ref, wv_ref, wo_ref, mask_ref,
    pick_ref, z_ref, att_ref, grad_ref, keep_ref, send_ref, q_ref, k_ref, v_ref, o_ref, other_ref,
):
    for w_ref, p_ref in ((wq_ref, q_ref), (wk_ref, k_ref), (wv_ref, v_ref)):
        p_ref[...] = nn(scaled_ref[...], w_ref[...]).astype(BF16)
    o_ref[...] = nt(up_ref[...], wo_ref[...]).astype(BF16)

    wide = (WIN, QUADS * WIN)
    key = lax.broadcasted_iota(jnp.int32, wide, 0)
    query = lax.broadcasted_iota(jnp.int32, wide, 1)
    same = query == key
    for h in range(1, QUADS):
        same = same | (query == key + h * WIN)
    other_ref[...] = jnp.where(same, 0.0, 1.0)
    lane = lax.broadcasted_iota(jnp.int32, (WIN, GW), 1)
    mine = [(lane >= HEAD * h) & (lane < HEAD * h + HEAD) for h in range(QUADS)]
    zero = jnp.zeros((WIN, GW), BF16)

    def by_head(a):
        return jnp.concatenate([jnp.where(m, a, zero) for m in mine], axis=0)

    def own_head(a):
        total = a[:WIN]
        for h in range(1, QUADS):
            total = jnp.where(mine[h], a[h * WIN : h * WIN + WIN], total)
        return total

    def window(i, _):
        at = pl.ds(pl.multiple_of(i * WIN, WIN), WIN)
        k, v = k_ref[at, :], v_ref[at, :]
        q, o = by_head(q_ref[at, :]), by_head(o_ref[at, :])
        scores = nt(k, q) * (SCALE * LOG2E) + other_ref[...] * mask_ref[at, :]
        raised = jnp.exp2(scores - jnp.max(scores, axis=0, keepdims=True))
        prob = raised * (1.0 / jnp.sum(raised, axis=0, keepdims=True))
        prob_half = prob.astype(BF16)
        prob_grad = nt(v, o)
        inner = jnp.sum(prob * prob_grad, axis=0, keepdims=True)
        score_grad = (prob * (prob_grad - inner)).astype(BF16)
        att_ref[at, :] = own_head(nn(prob_half.T, v)).astype(BF16)
        grad_ref[at, 0:GW] = (own_head(nn(score_grad.T, k)) * SCALE).astype(BF16)
        grad_ref[at, GW : 2 * GW] = (nn(score_grad, q) * SCALE).astype(BF16)
        grad_ref[at, 2 * GW : 3 * GW] = nn(prob_half, o).astype(BF16)
        return 0

    lax.fori_loop(0, WINS, window, 0)

    def weights(i, _):
        at = pl.ds(pl.multiple_of(i * 256, 256), 256)
        keep_ref[at, 0 : 3 * GW] = nn(scaled_t_ref[at, :], grad_ref[...])
        far = pl.ds(pl.multiple_of(i * 256 + 512, 256), 256)
        send_ref[at, 0 : 3 * GW] = nn(scaled_t_ref[far, :], grad_ref[...])
        return 0

    lax.fori_loop(0, 2, weights, 0)

    turned = nt(pick_ref[...], att_ref[...]).astype(BF16)
    for e in range(4):
        cols = pl.ds(pl.multiple_of((z_ref[0] ^ e) * GW, GW), GW)
        part = nn(turned, up_ref[:, cols])
        for y in range(4):
            at = 128 * y + 32 * e
            keep_ref[at : at + 32, 3 * GW :] = part[32 * y : 32 * y + 32]
            send_ref[at : at + 32, 3 * GW :] = part[128 + 32 * y : 160 + 32 * y]


def attend(g, scaled, scaled_t, up, qkv_weight, out_weight, mask, pick, z, after=()):
    full = lambda shape: pl.BlockSpec(shape, lambda i: (0, 0))
    return pl.pallas_call(
        behind(attend_kernel, len(after), 10),
        grid=(1,),
        out_shape=(
            jax.ShapeDtypeStruct((TOK, GW), BF16),
            jax.ShapeDtypeStruct((TOK, 3 * GW), BF16),
            jax.ShapeDtypeStruct((D // 2, 4 * GW), F32),
            jax.ShapeDtypeStruct((D // 2, 4 * GW), F32),
        ),
        in_specs=[
            full((TOK, D)),
            full((D, TOK)),
            full((TOK, D)),
            pl.BlockSpec((D, GW), lambda i: (0, g)),
            pl.BlockSpec((D, GW), lambda i: (0, GROUPS + g)),
            pl.BlockSpec((D, GW), lambda i: (0, 2 * GROUPS + g)),
            pl.BlockSpec((GW, D), lambda i: (g, 0)),
            full((TOK, 1)),
            full((GW, GW)),
            pl.BlockSpec(memory_space=pltpu.SMEM),
        ]
        + waits(after),
        out_specs=(
            full((TOK, GW)),
            full((TOK, 3 * GW)),
            full((D // 2, 4 * GW)),
            full((D // 2, 4 * GW)),
        ),
        scratch_shapes=[pltpu.VMEM((TOK, GW), BF16)] * 4 + [pltpu.VMEM((WIN, QUADS * WIN), F32)],
        compiler_params=params(62),
        cost_estimate=cost(8e9, 15e6),
        name="attend",
    )(scaled, scaled_t, up, qkv_weight, qkv_weight, qkv_weight, out_weight, mask, pick, z, *after)


def gate_kernel(out_ref):
    out_ref[...] = jnp.zeros((8, 128), F32)


def gate(passed, after):
    return pl.pallas_call(
        behind(gate_kernel, len(passed) + len(after), 0, len(passed)),
        out_shape=(jax.ShapeDtypeStruct((8, 128), F32),)
        + tuple(jax.ShapeDtypeStruct(p.shape, p.dtype) for p in passed),
        in_specs=waits(passed) + waits(after),
        out_specs=tuple(vmem(1) + waits(passed)),
        input_output_aliases={i: 1 + i for i in range(len(passed))},
        compiler_params=params(4),
        cost_estimate=cost(0, 1e4),
        name="gate",
    )(*passed, *after)[1:]


def block_kernel(a0, a1, a2, a3, x_ref, w_ref, out_ref):
    def rows(i, _):
        at = pl.ds(pl.multiple_of(i * 432, 432), 432)
        total = x_ref[at, :].astype(F32)
        for g, a in enumerate((a0, a1, a2, a3)):
            total = total + nn(a[at, :], w_ref[GW * g : GW * g + GW, :])
        out_ref[at, :] = total.astype(BF16)
        return 0

    lax.fori_loop(0, 2, rows, 0)


def block_sum(att, x, out_weight, after):
    return pl.pallas_call(
        behind(block_kernel, len(after), 6),
        out_shape=jax.ShapeDtypeStruct((TOK, D), BF16),
        in_specs=vmem(6) + waits(after),
        out_specs=vmem(1)[0],
        compiler_params=params(62),
        cost_estimate=cost(2e9, 8e6),
        name="block_sum",
    )(*att, x, out_weight, *after)


def product_kernel(g0, g1, g2, g3, w_ref, n_ref):
    def product(i, _):
        at = pl.ds(pl.multiple_of(i * 432, 432), 432)
        total = None
        for g, d in enumerate((g0, g1, g2, g3)):
            for part in range(3):
                base = part * D + g * GW
                piece = nt(d[at, part * GW : part * GW + GW], w_ref[:, base : base + GW])
                total = piece if total is None else total + piece
        n_ref[at, :] = total
        return 0

    lax.fori_loop(0, 2, product, 0)


def product(grads, qkv_weight, after=()):
    return pl.pallas_call(
        behind(product_kernel, len(after), 5),
        out_shape=jax.ShapeDtypeStruct((TOK, D), F32),
        in_specs=vmem(5) + waits(after),
        out_specs=vmem(1)[0],
        compiler_params=params(62),
        cost_estimate=cost(6e9, 15e6),
        name="product",
    )(*grads, qkv_weight, *after)


def leave_kernel(s_ref, x_ref, up_ref, gain_ref, mix_ref, out_ref, n_ref, sum_ref):
    step = pl.program_id(0)

    @pl.when(step == 0)
    def _():
        sum_ref[...] = jnp.zeros((8, D), F32)

    def rows(i, gain_sum):
        at = pl.ds(pl.multiple_of(i * 48, 48), 48)
        normed, inv_scale = norm_parts(x_ref[at, :].astype(F32))
        n = s_ref[at, :]
        both = n * normed
        gain = gain_ref[...]
        g = n * gain
        mean_g = jnp.sum(g, axis=-1, keepdims=True) * (1.0 / D)
        mean_gn = jnp.sum(both * gain, axis=-1, keepdims=True) * (1.0 / D)
        n_ref[at, :] = up_ref[at, :].astype(F32) + inv_scale * (g - mean_g - normed * mean_gn)
        return gain_sum + jnp.sum(both.reshape(6, 8, D), axis=0)

    gain_sum = lax.fori_loop(0, 6, rows, sum_ref[...])
    sum_ref[...] = gain_sum

    low = lax.broadcasted_iota(jnp.int32, (WIN, 128), 1) < HEAD
    to = pl.ds(pl.multiple_of(step * WIN, WIN), WIN)
    for p in range(8):
        cols = slice(128 * p, 128 * p + 128)
        level0 = jnp.concatenate([n_ref[0:HALF, cols], n_ref[WIN : WIN + HALF, cols]], axis=0)
        level1 = jnp.concatenate([n_ref[HALF:WIN, cols], n_ref[WIN + HALF : 2 * WIN, cols]], axis=0)
        out_ref[2 * p, to] = jnp.where(low, level0, pltpu.roll(level1, HEAD, 1)).astype(BF16)
        out_ref[2 * p + 1, to] = jnp.where(low, pltpu.roll(level0, HEAD, 1), level1).astype(BF16)

    @pl.when(step == 2)
    def _():
        whole = jnp.sum(gain_sum, axis=0, keepdims=True)
        high = whole.astype(BF16).astype(F32)
        mid = (whole - high).astype(BF16).astype(F32)
        row16 = lax.broadcasted_iota(jnp.int32, (16, D), 0)
        split = jnp.where(row16 == 0, high, jnp.where(row16 == 1, mid, whole - high - mid))
        split = jnp.where(row16 < 3, split, 0.0).astype(BF16)
        split = nn(split, mix_ref[...]).astype(BF16)
        for k in range(16):
            out_ref[k, 6 * HALF :] = split[:, 128 * (k // 2) : 128 * (k // 2) + 128]


def leave(norm_grad, x, up, gain, mix, after=()):
    full = lambda shape: pl.BlockSpec(shape, lambda i: (0,) * len(shape))
    part = pl.BlockSpec((2 * WIN, D), lambda i: (i, 0))
    return pl.pallas_call(
        behind(leave_kernel, len(after), 5),
        grid=(3,),
        out_shape=jax.ShapeDtypeStruct((16, ROWS, 128), BF16),
        in_specs=[part, part, part, full((1, D)), full((D, D))] + waits(after),
        out_specs=full((16, ROWS, 128)),
        scratch_shapes=[pltpu.VMEM((2 * WIN, D), F32), pltpu.VMEM((8, D), F32)],
        compiler_params=params(62),
        cost_estimate=cost(4e9, 10e6),
        name="leave",
    )(norm_grad, x, up, gain, mix, *after)


def join_kernel(r_ref, out_ref, gain_ref, s_ref, t_ref):
    gain = None
    for k in range(16):
        s_ref[k] = r_ref[k, 0 : 6 * HALF].astype(F32)
        term = r_ref[k, 6 * HALF :].astype(F32)
        gain = term if gain is None else gain + term
    gain_ref[...] = jnp.sum(gain, axis=0, keepdims=True)
    same = lax.broadcasted_iota(jnp.int32, (128, 128), 0) == lax.broadcasted_iota(
        jnp.int32, (128, 128), 1
    )
    same = same.astype(BF16)
    for r in range(12):
        for v in range(48):
            at = ((r // 6) * 3 + v % 3) * HALF + (r % 6) * 12
            to = 12 * v + SHIFT
            if to + 12 <= LON:
                t_ref[to : to + 12, :] = s_ref[v // 3, at : at + 12, :]
            else:
                t_ref[to:LON, :] = s_ref[v // 3, at : at + LON - to, :]
                t_ref[0 : to + 12 - LON, :] = s_ref[v // 3, at + LON - to : at + 12, :]
        turned = nt(same, t_ref[...].astype(BF16)).astype(BF16)
        out_ref[0, r] = turned[:HEAD]
        out_ref[1, r] = turned[HEAD:]


def join_pieces(pieces, passed, after):
    after = tuple(passed) + tuple(after)
    return pl.pallas_call(
        behind(join_kernel, len(after), 1, len(passed), 2),
        out_shape=(
            jax.ShapeDtypeStruct((2, 12, HEAD, LON), BF16),
            jax.ShapeDtypeStruct((1, 128), F32),
        )
        + tuple(jax.ShapeDtypeStruct(p.shape, p.dtype) for p in passed),
        in_specs=vmem(1) + waits(after),
        out_specs=tuple(vmem(2) + waits(passed)),
        input_output_aliases={1 + i: 2 + i for i in range(len(passed))},
        scratch_shapes=[pltpu.VMEM((16, 6 * HALF, 128), F32), pltpu.VMEM((LON, 128), F32)],
        compiler_params=params(62),
        cost_estimate=cost(2e9, 4e6),
        name="join_pieces",
    )(pieces, *after)


def device_index(x, y, z, core):
    return ((z * 2 + x % 2) * 4 + y) * 4 + (x // 2) * 2 + core


def swapped(z=0, x=0, y=0, core=0):
    pairs = []
    for px in range(4):
        for py in range(4):
            for pz in range(4):
                for c in range(2):
                    to = device_index(px ^ x, py ^ y, pz ^ z, c ^ core)
                    pairs.append((device_index(px, py, pz, c), to))
    return sorted(pairs)


class Sum:
    def __init__(self, keep, got):
        self.tail = (8, keep.shape[-1])
        self.spots = {n: (0, 1, 2, 3) for n in "yzx"}
        self.whole = {n: {e: e for e in range(4)} for n in "yzx"}
        self.terms = [(keep.reshape((4, 4, 4) + self.tail), self.whole, 0)]
        self.terms.append((got.reshape((4, 4, 4) + self.tail), self.whole, 0))

    def columns(self, low, high):
        part = Sum.__new__(Sum)
        part.tail, part.whole, part.spots = (8, high - low), self.whole, dict(self.spots)
        part.terms = [(a, places, low) for a, places, _ in self.terms]
        return part

    def cut(self, name, chosen):
        total = None
        spots = dict(self.spots)
        spots[name] = chosen
        for array, places, low in self.terms:
            index = tuple(
                slice(places[n][spots[n][0]], places[n][spots[n][-1]] + 1) for n in "yzx"
            )
            piece = array[index + (slice(None), slice(low, low + self.tail[1]))]
            total = piece if total is None else total + piece
        return total

    def offer(self, name, by):
        if len(self.spots[name]) == 4:
            give, rest = ((1, 2), (0, 3)) if by == 1 else ((2, 3), (0, 1))
        else:
            give, rest = (by,), (0,)
        piece = self.cut(name, give)
        self.spots[name] = rest
        places = {n: {e: i for i, e in enumerate(self.spots[n])} for n in "yzx"}
        places[name] = {e ^ by: i for i, e in enumerate(give)}
        return piece, places

    def ring_y(self, y, after=()):
        (keep, _, _), (got, _, _) = self.terms
        total = ordered_sum(keep, got, y, after)
        rest = total.reshape(4 * 128, self.tail[1])
        rest = lax.psum_scatter(rest, "lon", scatter_dimension=0, axis_index_groups=Y_RINGS, tiled=True)
        self.reduced = rest
        self.spots["y"] = (0,)
        places = dict(self.whole)
        places["y"] = {0: 0}
        self.terms = [(rest.reshape((1, 4, 4) + self.tail), places, 0)]
        return total

    def cells(self):
        found = []
        for array, places, low in self.terms:
            at = places["y"][0] * array.shape[1] + places["z"][0]
            found.append((array.reshape(-1, 32, array.shape[-1]), at, low // self.tail[1]))
        return found


Y_RINGS = [[c, c + 4, c + 8, c + 12] for c in range(4)]


def exchange(sums, name, by):
    offers = [s.offer(name, by) for s in sums]
    flat = [piece.reshape((-1,) + piece.shape[3:]) for piece, _ in offers]
    out = flat[0] if len(flat) == 1 else jnp.concatenate(flat, axis=-1)
    got = lax.ppermute(out, AXES, swapped(**{name: by}))
    at = 0
    for s, (piece, places) in zip(sums, offers):
        wide = piece.shape[-1]
        s.terms.append((got.reshape(piece.shape[:3] + (8, -1)), places, at))
        at += wide
    return out, got


def add_kernel(y_ref, a_ref, b_ref, *refs):
    out_ref = refs[-1]
    out_ref[...] = a_ref[...] + b_ref[...]


def ordered_sum(a, b, y, after):
    a, b = (t.reshape(4, 128, t.shape[-1]) for t in (a, b))
    block = (1,) + a.shape[1:]
    return pl.pallas_call(
        add_kernel,
        grid_spec=pltpu.PrefetchScalarGridSpec(
            num_scalar_prefetch=1,
            grid=(4,),
            in_specs=[pl.BlockSpec(block, lambda i, y: (i ^ y[0], 0, 0))] * 2 + waits(after),
            out_specs=pl.BlockSpec(block, lambda i, y: (i, 0, 0)),
        ),
        out_shape=jax.ShapeDtypeStruct(a.shape, F32),
        compiler_params=params(16),
        cost_estimate=cost(0, 5e6),
        name="ordered_sum",
    )(y, a, b, *after)


def last_cut_kernel(counts, *refs):
    ins, gain_ref, outs = refs[: sum(counts)], refs[sum(counts)], refs[sum(counts) + 1 :]
    at, col = 0, 0
    for n in counts:
        total = ins[at][0]
        for r in ins[at + 1 : at + n]:
            total = total + r[0]
        wide = total.shape[-1]
        for e in range(4):
            outs[e][:, col : col + wide] = total[8 * e : 8 * e + 8]
        at, col = at + n, col + wide
    row = lax.broadcasted_iota(jnp.int32, (8, 128), 0)
    outs[1][:, col:] = jnp.where(row == 0, gain_ref[...], 0.0)


def last_cut(parts, gain):
    cells = [t.cells() for t in parts]
    counts = tuple(len(c) for c in cells)
    widths = [t.tail[1] for t, c in zip(parts, cells) for _ in c]
    cells = sum(cells, [])
    whole = lambda shape: pl.BlockSpec(shape, lambda i: (0, 0))
    wide = [4 * D, 4 * D + 128, 4 * D, 4 * D]
    return pl.pallas_call(
        functools.partial(last_cut_kernel, counts),
        grid=(1,),
        in_specs=[
            pl.BlockSpec((1, 32, wide), functools.partial(lambda at, col, i: (at, 0, col), at, col))
            for (_, at, col), wide in zip(cells, widths)
        ]
        + [whole((1, 128))],
        out_specs=tuple(whole((8, w)) for w in wide),
        out_shape=tuple(jax.ShapeDtypeStruct((8, w), F32) for w in wide),
        compiler_params=params(24),
        cost_estimate=cost(0, 5e6),
        name="last_cut",
    )(*[a for a, _, _ in cells], gain)


def quarter_kernel(own, got1, got2, got3, gain_ref, z_ref, out_ref, s0, s1, s2, s3, q_ref):
    total = own[...] + got1[:, : 4 * D] + got2[...] + got3[...]
    for g in range(GROUPS):
        for part in range(3):
            at = part * D + g * GW
            out_ref[:, at : at + GW] = total[:, g * D + part * GW : g * D + part * GW + GW]
        q_ref[g] = total[:, g * D + 3 * GW : g * D + D]
    gain = jnp.broadcast_to(gain_ref[...] + got1[0:1, 4 * D :], (8, 128))
    for d, send in enumerate((s0, s1, s2, s3)):
        send[:, :GW] = q_ref[z_ref[0] ^ d]
        send[:, GW:] = gain


def quarters_of(own, got, gain, z):
    return pl.pallas_call(
        quarter_kernel,
        out_shape=(jax.ShapeDtypeStruct((8, 3 * D), F32),)
        + (jax.ShapeDtypeStruct((8, GW + 128), F32),) * 4,
        in_specs=vmem(5) + [pl.BlockSpec(memory_space=pltpu.SMEM)],
        out_specs=tuple(vmem(5)),
        scratch_shapes=[pltpu.VMEM((4, 8, GW), F32)],
        compiler_params=params(16),
        cost_estimate=cost(0, 1e6),
        name="quarters_of",
    )(own, *got, gain, z)


def gather_kernel(m0, m1, m2, m3, z_ref, out_ref, gain_ref, q_ref):
    gain = None
    for d, m in enumerate((m0, m1, m2, m3)):
        q_ref[d] = m[:, :GW]
        term = m[0:1, GW:]
        gain = term if gain is None else gain + term
    for e in range(4):
        out_ref[:, e * GW : e * GW + GW] = q_ref[z_ref[0] ^ e]
    gain_ref[...] = gain


def gather_quarters(pieces, z):
    return pl.pallas_call(
        gather_kernel,
        out_shape=(jax.ShapeDtypeStruct((8, D), F32), jax.ShapeDtypeStruct((1, 128), F32)),
        in_specs=vmem(4) + [pl.BlockSpec(memory_space=pltpu.SMEM)],
        out_specs=tuple(vmem(2)),
        scratch_shapes=[pltpu.VMEM((4, 8, GW), F32)],
        compiler_params=params(16),
        cost_estimate=cost(0, 1e6),
        name="gather_quarters",
    )(*pieces, z)


def row_picks():
    lat, lon = lax.axis_index("lat"), lax.axis_index("lon")
    z, xl = lat // 2, lat % 2
    y, xh, c = lon // 4, (lon // 2) % 2, lon % 2
    x = xh * 2 + xl
    i = jnp.arange(D, dtype=jnp.int32)
    tc = c ^ (i // 512)
    ty = y ^ ((i // 128) % 4)
    tz = z ^ ((i // 32) % 4)
    tx = x ^ ((i // 8) % 4)
    block = ((tz * 2 + tx % 2) * 4 + ty) * 4 + (tx // 2) * 2 + tc
    source = block * 8 + i % 8
    i = jnp.arange(GW, dtype=jnp.int32)
    tc = c ^ (i // 128)
    ty = y ^ ((i // 32) % 4)
    tx = x ^ ((i // 8) % 4)
    block = ((tx % 2) * 4 + ty) * 4 + (tx // 2) * 2 + tc
    group = block * 8 + i % 8
    return tuple(
        (t[:, None] == jnp.arange(t.shape[0], dtype=jnp.int32)[None, :]).astype(BF16)
        for t in (source, group)
    )


def gain_mix():
    i = jnp.arange(D, dtype=jnp.int32)
    source = ((i // 8) % 8) * 128 + (i // 64) * 8 + i % 8
    return (jnp.arange(D, dtype=jnp.int32)[:, None] == source[None, :]).astype(BF16)


def window_order(a):
    a = a.reshape((2, 2, 6, 3, 12) + a.shape[3:])
    return a.transpose((1, 3, 0, 2, 4) + tuple(range(5, a.ndim)))


def per_device(latents, land_mask, norm_gain, qkv_weight, out_weight, out_cotangent):
    lon_index = lax.axis_index("lon")
    pieces = split_pieces(latents.transpose(0, 1, 3, 2))
    pieces = lax.all_to_all(pieces, "lon", split_axis=0, concat_axis=0, tiled=True)
    pick, pick_group = row_picks()
    z_index = (lax.axis_index("lat") // 2).reshape(1)
    mask = jnp.roll(land_mask, -SHIFT, axis=2)
    mask = lax.dynamic_slice_in_dim(mask, lon_index * 36, 36, 2)
    mask = jnp.where(window_order(mask).reshape(TOK, 1) == 1, 0.0, -1e30).astype(F32)
    up = window_order(out_cotangent).reshape(TOK, D)
    gain = norm_gain.reshape(1, D)
    x, scaled, scaled_t = enter(pieces, gain, pick)
    y_index = (lon_index // 4).reshape(1)
    att, grads = [], []

    def heads(g, after):
        a, d, keep, send = attend(
            g, scaled, scaled_t, up, qkv_weight, out_weight, mask, pick_group, z_index, after
        )
        att.append(a)
        grads.append(d)
        return Sum(keep, lax.ppermute(send, AXES, swapped(core=1)))

    def newest(t):
        return t.terms[-1][0]

    s0 = heads(0, ())
    s1 = heads(1, ())
    total = s0.ring_y(y_index)
    s2 = heads(2, (total,))
    total = s1.ring_y(y_index, (att[2],))
    s3 = heads(3, (total, s0.reduced))
    norm_grad = product(grads, qkv_weight)
    total = s2.ring_y(y_index, (norm_grad,))
    s3.terms[-1] = (gate([newest(s3)], (norm_grad,))[0],) + s3.terms[-1][1:]
    s3, s4 = s3.columns(0, 2 * GW), s3.columns(2 * GW, 4 * GW)
    out3, _ = exchange([s3], "z", 1)
    out4, _ = exchange([s4], "z", 3)
    leaving = leave(norm_grad, x, up, gain, gain_mix(), (out3, out4, s1.reduced, total))
    back = lax.all_to_all(leaving, "lon", split_axis=0, concat_axis=0, tiled=True)
    def hand(sums, arrays):
        for t, p in zip(sums, arrays):
            t.terms[-1] = (p,) + t.terms[-1][1:]

    waiting = (s3, s4)
    passed = gate([newest(t) for t in waiting], (leaving,))
    block = block_sum(att, x, out_weight, (leaving,))
    hand(waiting, passed)
    exchange([s3], "z", 3)
    exchange([s4], "z", 1)
    exchange([s3, s4], "y", 1)
    exchange([s0, s1, s2], "z", 1)
    joined, gain_sum, one = join_pieces(back, (newest(s3),), (block,))
    hand((s3, s4), (one, one))
    exchange([s3, s4], "y", 3)
    exchange([s0, s1, s2], "z", 3)
    own, *send = last_cut((s0, s1, s2, s3, s4), gain_sum)
    got = [lax.ppermute(a, AXES, swapped(x=d)) for d, a in zip((1, 2, 3), send)]
    qkv_weight_grad, own, *send = quarters_of(own, got, gain_sum, z_index)
    got = [lax.ppermute(a, AXES, swapped(z=d)) for d, a in zip((1, 2, 3), send)]
    out_weight_grad, gain_sum = gather_quarters([own] + got, z_index)
    at = (lon_index % 2) * 64 + lax.axis_index("lat") * 8
    gain_grad = lax.dynamic_slice_in_dim(gain_sum.reshape(128), at, 8, 0)
    block = block.reshape(2, 3, 2, 6, 12, D).transpose(2, 0, 3, 1, 4, 5).reshape(2, 12, 36, D)
    latent_grad = joined.transpose(0, 1, 3, 2)
    return (block, latent_grad, qkv_weight_grad, out_weight_grad, gain_grad)


def solution(mesh):
    return jax.shard_map(
        per_device,
        mesh=mesh,
        in_specs=(
            P(None, "lat", None, "lon"),
            P(None, "lat", None),
            P(),
            P(),
            P(),
            P(None, "lat", "lon", None),
        ),
        out_specs=(
            P(None, "lat", "lon", None),
            P(None, "lat", None, "lon"),
            P(("lat", "lon"), None),
            P(("lat", "lon"), None),
            P(("lat", "lon")),
        ),
        check_vma=False,
    )
```

```python
import functools

import jax
import jax.numpy as jnp
from jax import lax
from jax.experimental import pallas as pl
from jax.experimental.pallas import tpu as pltpu
from jax.sharding import PartitionSpec as P

F32 = jnp.float32
BF16 = jnp.bfloat16
D = 1024
HEAD = 64
WIN = 144
HALF = 72
WINS = 6
TOK = WIN * WINS
SHIFT = 6
LON = 576
GROUPS = 4
ROWS = 6 * HALF + 16
GW = D // GROUPS
QUADS = GW // HEAD
SCALE = HEAD**-0.5
LOG2E = 1.4426950408889634
MIB = 1 << 20
AXES = ("lat", "lon")


def nn(a, b):
    return lax.dot_general(a, b, (((1,), (0,)), ((), ())), preferred_element_type=F32)


def nt(a, b):
    return lax.dot_general(a, b, (((1,), (1,)), ((), ())), preferred_element_type=F32)


def params(mib):
    return pltpu.CompilerParams(vmem_limit_bytes=mib * MIB)


def cost(flops, nbytes):
    return pl.CostEstimate(flops=int(flops / 10), bytes_accessed=int(nbytes / 10), transcendentals=0)


def waits(after):
    return [pl.BlockSpec(memory_space=pl.ANY)] * len(after)


def behind(kernel, count, operands, passed=0, results=1):
    def body(*refs):
        rest = refs[operands + count :]
        kernel(*refs[:operands], *rest[:results], *rest[results + passed :])

    return body


def vmem(n):
    return [pl.BlockSpec(memory_space=pltpu.VMEM)] * n


def split_kernel(z_ref, out_ref, t_ref, s_ref):
    row = lax.broadcasted_iota(jnp.int32, (LON, LON), 0)
    col = lax.broadcasted_iota(jnp.int32, (LON, LON), 1)
    source = row + SHIFT
    source = jnp.where(source >= LON, source - LON, source)
    pick = (col == source).astype(BF16)
    for r in range(12):
        both = jnp.concatenate([z_ref[0, r], z_ref[1, r]], axis=0)
        t_ref[...] = nt(pick, both)
        for v in range(48):
            at = ((r // 6) * 3 + v % 3) * HALF + (r % 6) * 12
            s_ref[v // 3, at : at + 12, :] = t_ref[12 * v : 12 * v + 12, :]
    for k in range(16):
        out_ref[k] = s_ref[k].astype(BF16)


def split_pieces(z):
    return pl.pallas_call(
        split_kernel,
        out_shape=jax.ShapeDtypeStruct((16, 6 * HALF, 128), BF16),
        in_specs=vmem(1),
        out_specs=vmem(1)[0],
        scratch_shapes=[pltpu.VMEM((LON, 128), F32), pltpu.VMEM((16, 6 * HALF, 128), F32)],
        compiler_params=params(62),
        cost_estimate=cost(2e9, 4e6),
        name="split_pieces",
    )(z)


def norm_parts(x):
    centred = x - jnp.sum(x, axis=-1, keepdims=True) * (1.0 / D)
    variance = jnp.sum(centred * centred, axis=-1, keepdims=True) * (1.0 / D)
    inv_scale = lax.rsqrt(variance + 1e-05)
    return centred * inv_scale, inv_scale


def enter_kernel(r_ref, gain_ref, pick_ref, x_ref, scaled_ref, scaled_t_ref, xs_ref):
    low = lax.broadcasted_iota(jnp.int32, (6 * HALF, 128), 1) < HEAD
    for p in range(8):
        first = r_ref[2 * p].astype(F32)
        second = r_ref[2 * p + 1].astype(F32)
        level0 = jnp.where(low, first, pltpu.roll(second, HEAD, 1))
        level1 = jnp.where(low, pltpu.roll(first, HEAD, 1), second)
        for w in range(WINS):
            at = w * WIN
            xs_ref[at : at + HALF, 128 * p : 128 * p + 128] = level0[HALF * w : HALF * w + HALF]
            xs_ref[at + HALF : at + WIN, 128 * p : 128 * p + 128] = level1[HALF * w : HALF * w + HALF]

    def rows(i, _):
        at = pl.ds(pl.multiple_of(i * 48, 48), 48)
        x = xs_ref[at, :]
        x_ref[at, :] = x.astype(BF16)
        normed, _ = norm_parts(x)
        scaled_ref[at, :] = (normed * gain_ref[...]).astype(BF16)
        return 0

    lax.fori_loop(0, TOK // 48, rows, 0)

    def turn(i, _):
        at = pl.ds(pl.multiple_of(i * 256, 256), 256)
        scaled_t_ref[at, :] = nt(pick_ref[at, :], scaled_ref[...]).astype(BF16)
        return 0

    lax.fori_loop(0, 4, turn, 0)


def enter(pieces, gain, pick):
    return pl.pallas_call(
        enter_kernel,
        out_shape=(
            jax.ShapeDtypeStruct((TOK, D), BF16),
            jax.ShapeDtypeStruct((TOK, D), BF16),
            jax.ShapeDtypeStruct((D, TOK), BF16),
        ),
        in_specs=vmem(3),
        out_specs=tuple(vmem(3)),
        scratch_shapes=[pltpu.VMEM((TOK, D), F32)],
        compiler_params=params(62),
        cost_estimate=cost(3e9, 9e6),
        name="enter",
    )(pieces, gain, pick)


def attend_kernel(
    scaled_ref, scaled_t_ref, up_ref, wq_ref, wk_ref, wv_ref, wo_ref, mask_ref,
    pick_ref, z_ref, att_ref, grad_ref, keep_ref, send_ref, q_ref, k_ref, v_ref, o_ref, other_ref,
):
    for w_ref, p_ref in ((wq_ref, q_ref), (wk_ref, k_ref), (wv_ref, v_ref)):
        p_ref[...] = nn(scaled_ref[...], w_ref[...]).astype(BF16)
    o_ref[...] = nt(up_ref[...], wo_ref[...]).astype(BF16)

    wide = (WIN, QUADS * WIN)
    key = lax.broadcasted_iota(jnp.int32, wide, 0)
    query = lax.broadcasted_iota(jnp.int32, wide, 1)
    same = query == key
    for h in range(1, QUADS):
        same = same | (query == key + h * WIN)
    other_ref[...] = jnp.where(same, 0.0, 1.0)
    lane = lax.broadcasted_iota(jnp.int32, (WIN, GW), 1)
    mine = [(lane >= HEAD * h) & (lane < HEAD * h + HEAD) for h in range(QUADS)]
    zero = jnp.zeros((WIN, GW), BF16)

    def by_head(a):
        return jnp.concatenate([jnp.where(m, a, zero) for m in mine], axis=0)

    def own_head(a):
        total = a[:WIN]
        for h in range(1, QUADS):
            total = jnp.where(mine[h], a[h * WIN : h * WIN + WIN], total)
        return total

    def window(i, _):
        at = pl.ds(pl.multiple_of(i * WIN, WIN), WIN)
        k, v = k_ref[at, :], v_ref[at, :]
        q, o = by_head(q_ref[at, :]), by_head(o_ref[at, :])
        scores = nt(k, q) * (SCALE * LOG2E) + other_ref[...] * mask_ref[at, :]
        raised = jnp.exp2(scores - jnp.max(scores, axis=0, keepdims=True))
        prob = raised * (1.0 / jnp.sum(raised, axis=0, keepdims=True))
        prob_half = prob.astype(BF16)
        prob_grad = nt(v, o)
        inner = jnp.sum(prob * prob_grad, axis=0, keepdims=True)
        score_grad = (prob * (prob_grad - inner)).astype(BF16)
        att_ref[at, :] = own_head(nn(prob_half.T, v)).astype(BF16)
        grad_ref[at, 0:GW] = (own_head(nn(score_grad.T, k)) * SCALE).astype(BF16)
        grad_ref[at, GW : 2 * GW] = (nn(score_grad, q) * SCALE).astype(BF16)
        grad_ref[at, 2 * GW : 3 * GW] = nn(prob_half, o).astype(BF16)
        return 0

    lax.fori_loop(0, WINS, window, 0)

    def weights(i, _):
        at = pl.ds(pl.multiple_of(i * 256, 256), 256)
        keep_ref[at, 0 : 3 * GW] = nn(scaled_t_ref[at, :], grad_ref[...])
        far = pl.ds(pl.multiple_of(i * 256 + 512, 256), 256)
        send_ref[at, 0 : 3 * GW] = nn(scaled_t_ref[far, :], grad_ref[...])
        return 0

    lax.fori_loop(0, 2, weights, 0)

    turned = nt(pick_ref[...], att_ref[...]).astype(BF16)
    for e in range(4):
        cols = pl.ds(pl.multiple_of((z_ref[0] ^ e) * GW, GW), GW)
        part = nn(turned, up_ref[:, cols])
        for y in range(4):
            at = 128 * y + 32 * e
            keep_ref[at : at + 32, 3 * GW :] = part[32 * y : 32 * y + 32]
            send_ref[at : at + 32, 3 * GW :] = part[128 + 32 * y : 160 + 32 * y]


def attend(g, scaled, scaled_t, up, qkv_weight, out_weight, mask, pick, z, after=()):
    full = lambda shape: pl.BlockSpec(shape, lambda i: (0, 0))
    return pl.pallas_call(
        behind(attend_kernel, len(after), 10),
        grid=(1,),
        out_shape=(
            jax.ShapeDtypeStruct((TOK, GW), BF16),
            jax.ShapeDtypeStruct((TOK, 3 * GW), BF16),
            jax.ShapeDtypeStruct((D // 2, 4 * GW), F32),
            jax.ShapeDtypeStruct((D // 2, 4 * GW), F32),
        ),
        in_specs=[
            full((TOK, D)),
            full((D, TOK)),
            full((TOK, D)),
            pl.BlockSpec((D, GW), lambda i: (0, g)),
            pl.BlockSpec((D, GW), lambda i: (0, GROUPS + g)),
            pl.BlockSpec((D, GW), lambda i: (0, 2 * GROUPS + g)),
            pl.BlockSpec((GW, D), lambda i: (g, 0)),
            full((TOK, 1)),
            full((GW, GW)),
            pl.BlockSpec(memory_space=pltpu.SMEM),
        ]
        + waits(after),
        out_specs=(
            full((TOK, GW)),
            full((TOK, 3 * GW)),
            full((D // 2, 4 * GW)),
            full((D // 2, 4 * GW)),
        ),
        scratch_shapes=[pltpu.VMEM((TOK, GW), BF16)] * 4 + [pltpu.VMEM((WIN, QUADS * WIN), F32)],
        compiler_params=params(62),
        cost_estimate=cost(8e9, 15e6),
        name="attend",
    )(scaled, scaled_t, up, qkv_weight, qkv_weight, qkv_weight, out_weight, mask, pick, z, *after)


def gate_kernel(out_ref):
    out_ref[...] = jnp.zeros((8, 128), F32)


def gate(passed, after):
    return pl.pallas_call(
        behind(gate_kernel, len(passed) + len(after), 0, len(passed)),
        out_shape=(jax.ShapeDtypeStruct((8, 128), F32),)
        + tuple(jax.ShapeDtypeStruct(p.shape, p.dtype) for p in passed),
        in_specs=waits(passed) + waits(after),
        out_specs=tuple(vmem(1) + waits(passed)),
        input_output_aliases={i: 1 + i for i in range(len(passed))},
        compiler_params=params(4),
        cost_estimate=cost(0, 1e4),
        name="gate",
    )(*passed, *after)[1:]


def block_kernel(a0, a1, a2, a3, x_ref, w_ref, out_ref):
    def rows(i, _):
        at = pl.ds(pl.multiple_of(i * 432, 432), 432)
        total = x_ref[at, :].astype(F32)
        for g, a in enumerate((a0, a1, a2, a3)):
            total = total + nn(a[at, :], w_ref[GW * g : GW * g + GW, :])
        out_ref[at, :] = total.astype(BF16)
        return 0

    lax.fori_loop(0, 2, rows, 0)


def block_sum(att, x, out_weight, after):
    return pl.pallas_call(
        behind(block_kernel, len(after), 6),
        out_shape=jax.ShapeDtypeStruct((TOK, D), BF16),
        in_specs=vmem(6) + waits(after),
        out_specs=vmem(1)[0],
        compiler_params=params(32),
        cost_estimate=cost(2e9, 8e6),
        name="block_sum",
    )(*att, x, out_weight, *after)


def product_kernel(g0, g1, g2, g3, w_ref, n_ref):
    def product(i, _):
        at = pl.ds(pl.multiple_of(i * 432, 432), 432)
        total = None
        for g, d in enumerate((g0, g1, g2, g3)):
            for part in range(3):
                base = part * D + g * GW
                piece = nt(d[at, part * GW : part * GW + GW], w_ref[:, base : base + GW])
                total = piece if total is None else total + piece
        n_ref[at, :] = total
        return 0

    lax.fori_loop(0, 2, product, 0)


def product(grads, qkv_weight, after=()):
    return pl.pallas_call(
        behind(product_kernel, len(after), 5),
        out_shape=jax.ShapeDtypeStruct((TOK, D), F32),
        in_specs=vmem(5) + waits(after),
        out_specs=vmem(1)[0],
        compiler_params=params(40),
        cost_estimate=cost(6e9, 15e6),
        name="product",
    )(*grads, qkv_weight, *after)


def leave_kernel(s_ref, x_ref, up_ref, gain_ref, mix_ref, out_ref, n_ref, sum_ref):
    step = pl.program_id(0)

    @pl.when(step == 0)
    def _():
        sum_ref[...] = jnp.zeros((8, D), F32)

    def rows(i, gain_sum):
        at = pl.ds(pl.multiple_of(i * 48, 48), 48)
        normed, inv_scale = norm_parts(x_ref[at, :].astype(F32))
        n = s_ref[at, :]
        both = n * normed
        gain = gain_ref[...]
        g = n * gain
        mean_g = jnp.sum(g, axis=-1, keepdims=True) * (1.0 / D)
        mean_gn = jnp.sum(both * gain, axis=-1, keepdims=True) * (1.0 / D)
        n_ref[at, :] = up_ref[at, :].astype(F32) + inv_scale * (g - mean_g - normed * mean_gn)
        return gain_sum + jnp.sum(both.reshape(6, 8, D), axis=0)

    gain_sum = lax.fori_loop(0, 6, rows, sum_ref[...])
    sum_ref[...] = gain_sum

    low = lax.broadcasted_iota(jnp.int32, (WIN, 128), 1) < HEAD
    to = pl.ds(pl.multiple_of(step * WIN, WIN), WIN)
    for p in range(8):
        cols = slice(128 * p, 128 * p + 128)
        level0 = jnp.concatenate([n_ref[0:HALF, cols], n_ref[WIN : WIN + HALF, cols]], axis=0)
        level1 = jnp.concatenate([n_ref[HALF:WIN, cols], n_ref[WIN + HALF : 2 * WIN, cols]], axis=0)
        out_ref[2 * p, to] = jnp.where(low, level0, pltpu.roll(level1, HEAD, 1)).astype(BF16)
        out_ref[2 * p + 1, to] = jnp.where(low, pltpu.roll(level0, HEAD, 1), level1).astype(BF16)

    @pl.when(step == 2)
    def _():
        whole = jnp.sum(gain_sum, axis=0, keepdims=True)
        high = whole.astype(BF16).astype(F32)
        mid = (whole - high).astype(BF16).astype(F32)
        row16 = lax.broadcasted_iota(jnp.int32, (16, D), 0)
        split = jnp.where(row16 == 0, high, jnp.where(row16 == 1, mid, whole - high - mid))
        split = jnp.where(row16 < 3, split, 0.0).astype(BF16)
        split = nn(split, mix_ref[...]).astype(BF16)
        for k in range(16):
            out_ref[k, 6 * HALF :] = split[:, 128 * (k // 2) : 128 * (k // 2) + 128]


def leave(norm_grad, x, up, gain, mix, after=()):
    full = lambda shape: pl.BlockSpec(shape, lambda i: (0,) * len(shape))
    part = pl.BlockSpec((2 * WIN, D), lambda i: (i, 0))
    return pl.pallas_call(
        behind(leave_kernel, len(after), 5),
        grid=(3,),
        out_shape=jax.ShapeDtypeStruct((16, ROWS, 128), BF16),
        in_specs=[part, part, part, full((1, D)), full((D, D))] + waits(after),
        out_specs=full((16, ROWS, 128)),
        scratch_shapes=[pltpu.VMEM((2 * WIN, D), F32), pltpu.VMEM((8, D), F32)],
        compiler_params=params(62),
        cost_estimate=cost(4e9, 10e6),
        name="leave",
    )(norm_grad, x, up, gain, mix, *after)


def join_kernel(r_ref, out_ref, gain_ref, s_ref, t_ref):
    gain = None
    for k in range(16):
        s_ref[k] = r_ref[k, 0 : 6 * HALF].astype(F32)
        term = r_ref[k, 6 * HALF :].astype(F32)
        gain = term if gain is None else gain + term
    gain_ref[...] = jnp.sum(gain, axis=0, keepdims=True)
    same = lax.broadcasted_iota(jnp.int32, (128, 128), 0) == lax.broadcasted_iota(
        jnp.int32, (128, 128), 1
    )
    same = same.astype(BF16)
    for r in range(12):
        for v in range(48):
            at = ((r // 6) * 3 + v % 3) * HALF + (r % 6) * 12
            to = 12 * v + SHIFT
            if to + 12 <= LON:
                t_ref[to : to + 12, :] = s_ref[v // 3, at : at + 12, :]
            else:
                t_ref[to:LON, :] = s_ref[v // 3, at : at + LON - to, :]
                t_ref[0 : to + 12 - LON, :] = s_ref[v // 3, at + LON - to : at + 12, :]
        turned = nt(same, t_ref[...].astype(BF16)).astype(BF16)
        out_ref[0, r] = turned[:HEAD]
        out_ref[1, r] = turned[HEAD:]


def join_pieces(pieces, passed, after):
    after = tuple(passed) + tuple(after)
    return pl.pallas_call(
        behind(join_kernel, len(after), 1, len(passed), 2),
        out_shape=(
            jax.ShapeDtypeStruct((2, 12, HEAD, LON), BF16),
            jax.ShapeDtypeStruct((1, 128), F32),
        )
        + tuple(jax.ShapeDtypeStruct(p.shape, p.dtype) for p in passed),
        in_specs=vmem(1) + waits(after),
        out_specs=tuple(vmem(2) + waits(passed)),
        input_output_aliases={1 + i: 2 + i for i in range(len(passed))},
        scratch_shapes=[pltpu.VMEM((16, 6 * HALF, 128), F32), pltpu.VMEM((LON, 128), F32)],
        compiler_params=params(62),
        cost_estimate=cost(2e9, 4e6),
        name="join_pieces",
    )(pieces, *after)


def device_index(x, y, z, core):
    return ((z * 2 + x % 2) * 4 + y) * 4 + (x // 2) * 2 + core


def swapped(z=0, x=0, y=0, core=0):
    pairs = []
    for px in range(4):
        for py in range(4):
            for pz in range(4):
                for c in range(2):
                    to = device_index(px ^ x, py ^ y, pz ^ z, c ^ core)
                    pairs.append((device_index(px, py, pz, c), to))
    return sorted(pairs)


class Sum:
    def __init__(self, keep, got):
        self.tail = (8, keep.shape[-1])
        self.spots = {n: (0, 1, 2, 3) for n in "yzx"}
        self.whole = {n: {e: e for e in range(4)} for n in "yzx"}
        self.terms = [(keep.reshape((4, 4, 4) + self.tail), self.whole, 0)]
        self.terms.append((got.reshape((4, 4, 4) + self.tail), self.whole, 0))

    def columns(self, low, high):
        part = Sum.__new__(Sum)
        part.tail, part.whole, part.spots = (8, high - low), self.whole, dict(self.spots)
        part.terms = [(a, places, low) for a, places, _ in self.terms]
        return part

    def cut(self, name, chosen):
        total = None
        spots = dict(self.spots)
        spots[name] = chosen
        for array, places, low in self.terms:
            index = tuple(
                slice(places[n][spots[n][0]], places[n][spots[n][-1]] + 1) for n in "yzx"
            )
            piece = array[index + (slice(None), slice(low, low + self.tail[1]))]
            total = piece if total is None else total + piece
        return total

    def offer(self, name, by):
        if len(self.spots[name]) == 4:
            give, rest = ((1, 2), (0, 3)) if by == 1 else ((2, 3), (0, 1))
        else:
            give, rest = (by,), (0,)
        piece = self.cut(name, give)
        self.spots[name] = rest
        places = {n: {e: i for i, e in enumerate(self.spots[n])} for n in "yzx"}
        places[name] = {e ^ by: i for i, e in enumerate(give)}
        return piece, places

    def ring_y(self, y, after=()):
        (keep, _, _), (got, _, _) = self.terms
        total = ordered_sum(keep, got, y, after)
        rest = total.reshape(4 * 128, self.tail[1])
        rest = lax.psum_scatter(rest, "lon", scatter_dimension=0, axis_index_groups=Y_RINGS, tiled=True)
        self.reduced = rest
        self.spots["y"] = (0,)
        places = dict(self.whole)
        places["y"] = {0: 0}
        self.terms = [(rest.reshape((1, 4, 4) + self.tail), places, 0)]
        return total

    def cells(self):
        found = []
        for array, places, low in self.terms:
            at = places["y"][0] * array.shape[1] + places["z"][0]
            found.append((array.reshape(-1, 32, array.shape[-1]), at, low // self.tail[1]))
        return found


Y_RINGS = [[c, c + 4, c + 8, c + 12] for c in range(4)]


def exchange(sums, name, by):
    offers = [s.offer(name, by) for s in sums]
    flat = [piece.reshape((-1,) + piece.shape[3:]) for piece, _ in offers]
    out = flat[0] if len(flat) == 1 else jnp.concatenate(flat, axis=-1)
    got = lax.ppermute(out, AXES, swapped(**{name: by}))
    at = 0
    for s, (piece, places) in zip(sums, offers):
        wide = piece.shape[-1]
        s.terms.append((got.reshape(piece.shape[:3] + (8, -1)), places, at))
        at += wide
    return out, got


def add_kernel(y_ref, a_ref, b_ref, *refs):
    out_ref = refs[-1]
    out_ref[...] = a_ref[...] + b_ref[...]


def ordered_sum(a, b, y, after):
    a, b = (t.reshape(4, 128, t.shape[-1]) for t in (a, b))
    block = (1,) + a.shape[1:]
    return pl.pallas_call(
        add_kernel,
        grid_spec=pltpu.PrefetchScalarGridSpec(
            num_scalar_prefetch=1,
            grid=(4,),
            in_specs=[pl.BlockSpec(block, lambda i, y: (i ^ y[0], 0, 0))] * 2 + waits(after),
            out_specs=pl.BlockSpec(block, lambda i, y: (i, 0, 0)),
        ),
        out_shape=jax.ShapeDtypeStruct(a.shape, F32),
        compiler_params=params(16),
        cost_estimate=cost(0, 5e6),
        name="ordered_sum",
    )(y, a, b, *after)


def last_cut_kernel(counts, *refs):
    ins, gain_ref, outs = refs[: sum(counts)], refs[sum(counts)], refs[sum(counts) + 1 :]
    at, col = 0, 0
    for n in counts:
        total = ins[at][0]
        for r in ins[at + 1 : at + n]:
            total = total + r[0]
        wide = total.shape[-1]
        for e in range(4):
            outs[e][:, col : col + wide] = total[8 * e : 8 * e + 8]
        at, col = at + n, col + wide
    row = lax.broadcasted_iota(jnp.int32, (8, 128), 0)
    outs[1][:, col:] = jnp.where(row == 0, gain_ref[...], 0.0)


def last_cut(parts, gain):
    cells = [t.cells() for t in parts]
    counts = tuple(len(c) for c in cells)
    widths = [t.tail[1] for t, c in zip(parts, cells) for _ in c]
    cells = sum(cells, [])
    whole = lambda shape: pl.BlockSpec(shape, lambda i: (0, 0))
    wide = [4 * D, 4 * D + 128, 4 * D, 4 * D]
    return pl.pallas_call(
        functools.partial(last_cut_kernel, counts),
        grid=(1,),
        in_specs=[
            pl.BlockSpec((1, 32, wide), functools.partial(lambda at, col, i: (at, 0, col), at, col))
            for (_, at, col), wide in zip(cells, widths)
        ]
        + [whole((1, 128))],
        out_specs=tuple(whole((8, w)) for w in wide),
        out_shape=tuple(jax.ShapeDtypeStruct((8, w), F32) for w in wide),
        compiler_params=params(24),
        cost_estimate=cost(0, 5e6),
        name="last_cut",
    )(*[a for a, _, _ in cells], gain)


def quarter_kernel(own, got1, got2, got3, gain_ref, z_ref, out_ref, s0, s1, s2, s3, q_ref):
    total = own[...] + got1[:, : 4 * D] + got2[...] + got3[...]
    for g in range(GROUPS):
        for part in range(3):
            at = part * D + g * GW
            out_ref[:, at : at + GW] = total[:, g * D + part * GW : g * D + part * GW + GW]
        q_ref[g] = total[:, g * D + 3 * GW : g * D + D]
    gain = jnp.broadcast_to(gain_ref[...] + got1[0:1, 4 * D :], (8, 128))
    for d, send in enumerate((s0, s1, s2, s3)):
        send[:, :GW] = q_ref[z_ref[0] ^ d]
        send[:, GW:] = gain


def quarters_of(own, got, gain, z):
    return pl.pallas_call(
        quarter_kernel,
        out_shape=(jax.ShapeDtypeStruct((8, 3 * D), F32),)
        + (jax.ShapeDtypeStruct((8, GW + 128), F32),) * 4,
        in_specs=vmem(5) + [pl.BlockSpec(memory_space=pltpu.SMEM)],
        out_specs=tuple(vmem(5)),
        scratch_shapes=[pltpu.VMEM((4, 8, GW), F32)],
        compiler_params=params(16),
        cost_estimate=cost(0, 1e6),
        name="quarters_of",
    )(own, *got, gain, z)


def gather_kernel(m0, m1, m2, m3, z_ref, out_ref, gain_ref, q_ref):
    gain = None
    for d, m in enumerate((m0, m1, m2, m3)):
        q_ref[d] = m[:, :GW]
        term = m[0:1, GW:]
        gain = term if gain is None else gain + term
    for e in range(4):
        out_ref[:, e * GW : e * GW + GW] = q_ref[z_ref[0] ^ e]
    gain_ref[...] = gain


def gather_quarters(pieces, z):
    return pl.pallas_call(
        gather_kernel,
        out_shape=(jax.ShapeDtypeStruct((8, D), F32), jax.ShapeDtypeStruct((1, 128), F32)),
        in_specs=vmem(4) + [pl.BlockSpec(memory_space=pltpu.SMEM)],
        out_specs=tuple(vmem(2)),
        scratch_shapes=[pltpu.VMEM((4, 8, GW), F32)],
        compiler_params=params(16),
        cost_estimate=cost(0, 1e6),
        name="gather_quarters",
    )(*pieces, z)


def row_picks():
    lat, lon = lax.axis_index("lat"), lax.axis_index("lon")
    z, xl = lat // 2, lat % 2
    y, xh, c = lon // 4, (lon // 2) % 2, lon % 2
    x = xh * 2 + xl
    i = jnp.arange(D, dtype=jnp.int32)
    tc = c ^ (i // 512)
    ty = y ^ ((i // 128) % 4)
    tz = z ^ ((i // 32) % 4)
    tx = x ^ ((i // 8) % 4)
    block = ((tz * 2 + tx % 2) * 4 + ty) * 4 + (tx // 2) * 2 + tc
    source = block * 8 + i % 8
    i = jnp.arange(GW, dtype=jnp.int32)
    tc = c ^ (i // 128)
    ty = y ^ ((i // 32) % 4)
    tx = x ^ ((i // 8) % 4)
    block = ((tx % 2) * 4 + ty) * 4 + (tx // 2) * 2 + tc
    group = block * 8 + i % 8
    return tuple(
        (t[:, None] == jnp.arange(t.shape[0], dtype=jnp.int32)[None, :]).astype(BF16)
        for t in (source, group)
    )


def gain_mix():
    i = jnp.arange(D, dtype=jnp.int32)
    source = ((i // 8) % 8) * 128 + (i // 64) * 8 + i % 8
    return (jnp.arange(D, dtype=jnp.int32)[:, None] == source[None, :]).astype(BF16)


def window_order(a):
    a = a.reshape((2, 2, 6, 3, 12) + a.shape[3:])
    return a.transpose((1, 3, 0, 2, 4) + tuple(range(5, a.ndim)))


def per_device(latents, land_mask, norm_gain, qkv_weight, out_weight, out_cotangent):
    lon_index = lax.axis_index("lon")
    pieces = split_pieces(latents.transpose(0, 1, 3, 2))
    pieces = lax.all_to_all(pieces, "lon", split_axis=0, concat_axis=0, tiled=True)
    pick, pick_group = row_picks()
    z_index = (lax.axis_index("lat") // 2).reshape(1)
    mask = jnp.roll(land_mask, -SHIFT, axis=2)
    mask = lax.dynamic_slice_in_dim(mask, lon_index * 36, 36, 2)
    mask = jnp.where(window_order(mask).reshape(TOK, 1) == 1, 0.0, -1e30).astype(F32)
    up = window_order(out_cotangent).reshape(TOK, D)
    gain = norm_gain.reshape(1, D)
    x, scaled, scaled_t = enter(pieces, gain, pick)
    y_index = (lon_index // 4).reshape(1)
    att, grads = [], []

    def heads(g, after):
        a, d, keep, send = attend(
            g, scaled, scaled_t, up, qkv_weight, out_weight, mask, pick_group, z_index, after
        )
        att.append(a)
        grads.append(d)
        return Sum(keep, lax.ppermute(send, AXES, swapped(core=1)))

    def newest(t):
        return t.terms[-1][0]

    s0 = heads(0, ())
    s1 = heads(1, ())
    total = s0.ring_y(y_index)
    s2 = heads(2, (total,))
    total = s1.ring_y(y_index, (att[2],))
    s3 = heads(3, (total, s0.reduced))
    total = s2.ring_y(y_index, (att[3],))
    norm_grad = product(grads, qkv_weight)
    s3, s4 = s3.columns(0, 2 * GW), s3.columns(2 * GW, 4 * GW)
    out3, _ = exchange([s3], "z", 1)
    out4, _ = exchange([s4], "z", 3)
    leaving = leave(norm_grad, x, up, gain, gain_mix(), (out3, out4, s1.reduced, total))
    back = lax.all_to_all(leaving, "lon", split_axis=0, concat_axis=0, tiled=True)
    def hand(sums, arrays):
        for t, p in zip(sums, arrays):
            t.terms[-1] = (p,) + t.terms[-1][1:]

    waiting = (s3, s4)
    passed = gate([newest(t) for t in waiting], (leaving,))
    block = block_sum(att, x, out_weight, (leaving,))
    hand(waiting, passed)
    exchange([s3], "z", 3)
    exchange([s4], "z", 1)
    exchange([s3, s4], "y", 1)
    exchange([s0, s1, s2], "z", 1)
    joined, gain_sum, one = join_pieces(back, (newest(s3),), (block,))
    hand((s3, s4), (one, one))
    exchange([s3, s4], "y", 3)
    exchange([s0, s1, s2], "z", 3)
    own, *send = last_cut((s0, s1, s2, s3, s4), gain_sum)
    got = [lax.ppermute(a, AXES, swapped(x=d)) for d, a in zip((1, 2, 3), send)]
    qkv_weight_grad, own, *send = quarters_of(own, got, gain_sum, z_index)
    got = [lax.ppermute(a, AXES, swapped(z=d)) for d, a in zip((1, 2, 3), send)]
    out_weight_grad, gain_sum = gather_quarters([own] + got, z_index)
    at = (lon_index % 2) * 64 + lax.axis_index("lat") * 8
    gain_grad = lax.dynamic_slice_in_dim(gain_sum.reshape(128), at, 8, 0)
    block = block.reshape(2, 3, 2, 6, 12, D).transpose(2, 0, 3, 1, 4, 5).reshape(2, 12, 36, D)
    latent_grad = joined.transpose(0, 1, 3, 2)
    return (block, latent_grad, qkv_weight_grad, out_weight_grad, gain_grad)


def solution(mesh):
    return jax.shard_map(
        per_device,
        mesh=mesh,
        in_specs=(
            P(None, "lat", None, "lon"),
            P(None, "lat", None),
            P(),
            P(),
            P(),
            P(None, "lat", "lon", None),
        ),
        out_specs=(
            P(None, "lat", "lon", None),
            P(None, "lat", None, "lon"),
            P(("lat", "lon"), None),
            P(("lat", "lon"), None),
            P(("lat", "lon")),
        ),
        check_vma=False,
    )
```
